256 devices in a mesh: sec: 4 (over z_hi), dp: 8 (over x, z_lo), mp: 8 (over y, core).
Axes of the slice: x: 4, y: 4, z: 8 (z_hi: 4, z_lo: 2; z = z_hi * 2 + z_lo), core: 2. Of those that a mesh axis runs over, the one named last changes fastest.
Arguments:
- cache_keys: bfloat16 [512, 1024, 1024], P(('sec', 'dp'), None, 'mp'), may hold values from -6 to 6
- cache_values: bfloat16 [512, 1024, 1024], P(('sec', 'dp'), None, 'mp'), may hold values from -6 to 6
- step_queries: bfloat16 [512, 4, 5120], P(('sec', 'dp'), None, 'mp'), may hold values from -6 to 6
- step_keys: bfloat16 [512, 4, 1024], P(('sec', 'dp'), None, 'mp'), may hold values from -6 to 6
- step_values: bfloat16 [512, 4, 1024], P(('sec', 'dp'), None, 'mp'), may hold values from -6 to 6
- reward_head: bfloat16 [5120], P('mp'), may hold values from -0.25 to 0.25
- lengths: int32 [512], replicated, may hold values from 1 to 24, 6144 in all
- assign: int32 [512], replicated, may hold values from 0 to 511, as said below
- response_feats: bfloat16 [512, 24, 5120], P(('sec', 'dp'), None, 'mp'), may hold values from -6 to 6
- out_proj: bfloat16 [5120, 5120], P(('sec', 'dp'), 'mp'), may hold values from -0.078125 to 0.078125
- loss_probe: bfloat16 [5120], replicated, may hold values from -4 to 4
Outputs:
- advantages: float32 [512], replicated
- grad_features: bfloat16 [512, 24, 5120], P(('sec', 'dp'), None, 'mp')
- grad_proj: float32 [5120, 5120], P(('sec', 'dp'), 'mp')
The draws below stay inside these ranges and needn't reach their ends.
Inputs may be any that keep to these rules, and one draw needn't show every extreme that they name: assign is a permutation of 0 to 511; slot q lies on learner shard q // 16; the 16 rows r with the same r // 16 go to 16 different learner shards (at most 1 row on any shard).
All inputs are finite; a program needn't handle non-finite values.
Results may differ from the reference program's by a relative error of at most 0.0075.
Values may be sent and summed in bfloat16 or wider, within the bound.
No kernel may reach another device: no remote copies, remote signals or barrier semaphores. Data moves between devices by JAX's collectives and lax.ppermute only.
A program may use at most 128 MiB of HBM per device.

```python
import math
import jax
import jax.numpy as jnp
import numpy as np
from jax import lax

D = 5120
H = 40
KVH = 8
HD = 128
ATTN = 5120
CTX = 1024
STEPS = 4
ROWS_DEV = 16
RESP = 24
GROUP = 16
SHARDS = 32
ROWS = 512


def drawn_parts(key):
    direction = jax.random.rademacher(jax.random.fold_in(key, 91), (HD,), jnp.float32)
    offset = jax.random.randint(jax.random.fold_in(key, 92), (), 0, 4)
    marked = (jnp.arange(ROWS) + offset) % 4 == 0
    return (direction, marked)


def draw_step_queries(key, part):
    direction, marked = drawn_parts(key)
    key = jax.random.fold_in(key, 11)
    strength_key, jitter_key = jax.random.split(key)
    strength = jax.random.uniform(strength_key, (ROWS, STEPS, H, 1), jnp.float32, 2.5, 5.0)
    jitter = jax.random.normal(jitter_key, (ROWS, STEPS, H, HD), jnp.float32)
    aligned = strength * direction + 0.3 * jitter
    queries = jnp.where(marked[:, None, None, None], aligned, jitter)
    return jnp.clip(queries, -6.0, 6.0).reshape(ROWS, STEPS, H * HD).astype(jnp.bfloat16)


def draw_cache_keys(key, part):
    direction, marked = drawn_parts(key)
    key = jax.random.fold_in(key, 13)
    first_key, spacing_key, jitter_key = jax.random.split(key, 3)
    first_slot = jax.random.randint(first_key, (ROWS, 1, KVH, 1), 0, CTX)
    second_slot = (first_slot + jax.random.randint(spacing_key, (ROWS, 1, KVH, 1), 1, CTX)) % CTX
    positions = jnp.arange(CTX)[None, :, None, None]
    top_strength = 4.5
    jitter = jax.random.normal(jitter_key, (ROWS, CTX, KVH, HD), jnp.float32)
    spacing = 2.0 / (math.sqrt(HD) * 3.75)
    marked_rows = marked[:, None, None, None]
    key_table = jnp.where(marked_rows & (positions == first_slot), top_strength * direction, jitter)
    key_table = jnp.where(marked_rows & (positions == second_slot), (top_strength - spacing) * direction, key_table)
    return jnp.clip(key_table, -6.0, 6.0).reshape(ROWS, CTX, KVH * HD).astype(jnp.bfloat16)


def draw_assign(key, part):
    key = jax.random.fold_in(key, 7)
    spread = min(ROWS_DEV, SHARDS)
    shuffled = jax.random.permutation(key, SHARDS).astype(jnp.int32)
    position = jnp.argsort(shuffled, stable=True).astype(jnp.int32)
    values = jnp.arange(SHARDS, dtype=jnp.int32)
    priority = jnp.where(values == 1, -2, jnp.where(values == SHARDS // 2, -1, position))
    offsets = jnp.argsort(priority, stable=True).astype(jnp.int32)[:spread]
    source = jnp.arange(SHARDS, dtype=jnp.int32)[:, None]
    within = jnp.arange(ROWS_DEV, dtype=jnp.int32)[None, :]
    target = (source + offsets[within % spread]) % SHARDS
    return (target * ROWS_DEV + within).reshape(-1).astype(jnp.int32)


def shard_levels(stream_key, dims, shards, least, largest):
    def one(dim, blocks):
        heights = jax.random.uniform(jax.random.fold_in(jax.random.fold_in(stream_key, 6), dim), (blocks,), jnp.float32, least / len(shards), largest / len(shards))
        return jnp.repeat(jnp.exp(heights), dims[dim] // blocks).reshape((-1,) + (1,) * (len(dims) - dim - 1))

    factor_of = one(*shards[0])
    for cut in shards[1:]:
        factor_of = factor_of * one(*cut)
    return factor_of


def profile(count, total, most, slope):
    loads = [(1 << 20) // math.isqrt(rank ** slope) + 1 for rank in range(2, count + 1)]
    spare, given = total - most - (count - 1), [1] * (count - 1)
    while spare > 0:
        free = [i for i in range(count - 1) if given[i] < most]
        whole, remaining = sum([loads[i] for i in free]), spare
        for i in free:
            more = min(most - given[i], max(1, remaining * loads[i] // whole), spare)
            given[i] = given[i] + more
            spare = spare - more
    return np.array([most] + given)


def uneven(rng, amount, total, most, lean):
    if amount == 2:
        one = jax.random.randint(rng, (), max(1, total - most), min(most, total - 1) + 1)
        return jnp.stack([one, total - one])
    sizes = jnp.asarray(profile(amount, total, most, lean), jnp.int32)
    twos = (amount - 1) // 2
    giver, sink = sizes[1:1 + 2 * twos:2], sizes[2:2 + 2 * twos:2]
    room = jnp.minimum(giver - 1, most - sink)
    passed = jax.random.randint(jax.random.fold_in(rng, 1), (twos,), 0, 1 << 20) % (room + 1)
    sizes = sizes.at[1:1 + 2 * twos:2].set(giver - passed).at[2:2 + 2 * twos:2].set(sink + passed)
    return sizes[jax.random.permutation(jax.random.fold_in(rng, 2), amount)]


def gaussian(rng, dims, scale, most, cuts=(), kind=jnp.bfloat16):
    values = jax.random.normal(rng, dims, jnp.float32) * scale
    if len(cuts) > 0:
        values = shard_levels(rng, dims, cuts, -0.22, 0.18) * values
    return jnp.clip(values, min=-most, max=most).astype(kind)


def setup_inputs(seed: int = 0) -> dict:
    streams_of = jax.random.split(jax.random.key(seed), 12)
    return {
        "cache_keys": draw_cache_keys(jax.random.fold_in(streams_of[11], 71), 0),
        "cache_values": gaussian(streams_of[1], (ROWS, CTX, KVH * HD), 1.0, 6.0, ((0, 32), (2, 8))),
        "step_queries": draw_step_queries(jax.random.fold_in(streams_of[11], 71), 0),
        "step_keys": gaussian(streams_of[3], (ROWS, STEPS, KVH * HD), 1.0, 6.0, ((0, 32), (2, 8))),
        "step_values": gaussian(streams_of[4], (ROWS, STEPS, KVH * HD), 1.0, 6.0, ((0, 32), (2, 8))),
        "reward_head": gaussian(streams_of[5], (ATTN,), (ATTN // 8) ** -0.5, 0.25, ((0, 8),)),
        "lengths": uneven(streams_of[6], ROWS, ROWS * RESP // 2, RESP, 0).astype(jnp.int32),
        "assign": draw_assign(jax.random.fold_in(streams_of[11], 71), 0),
        "response_feats": gaussian(streams_of[8], (ROWS, RESP, ATTN), 1.0, 6.0, ((0, 32), (2, 8))),
        "out_proj": gaussian(streams_of[9], (D, ATTN), ATTN ** -0.5, 0.078125, ((0, 32), (1, 8))),
        "loss_probe": gaussian(streams_of[10], (D,), 1.0, 4.0),
    }


def decode_rows(step_queries, cache_keys, cache_values, step_keys, step_values):
    rows = step_queries.shape[0]
    kv_local = cache_keys.shape[2] // HD
    heads_local = step_queries.shape[2] // HD
    share = heads_local // kv_local
    context = cache_keys.shape[1]
    queries = step_queries.reshape(rows, STEPS, kv_local, share, HD).astype(jnp.float32)
    keys_far = cache_keys.reshape(rows, context, kv_local, HD).astype(jnp.float32)
    values_far = cache_values.reshape(rows, context, kv_local, HD).astype(jnp.float32)
    keys_near = step_keys.reshape(rows, STEPS, kv_local, HD).astype(jnp.float32)
    values_near = step_values.reshape(rows, STEPS, kv_local, HD).astype(jnp.float32)
    scale = 1.0 / math.sqrt(HD)
    far = jnp.einsum('rskgh,rckh->rksgc', queries, keys_far) * scale
    near = jnp.einsum('rskgh,rjkh->rksgj', queries, keys_near) * scale
    causal = (jnp.arange(STEPS)[None, :] <= jnp.arange(STEPS)[:, None])[None, None, :, None, :]
    near = jnp.where(causal, near, -jnp.inf)
    top = jnp.maximum(far.max(-1), near.max(-1))[..., None]
    far_exp = jnp.exp(far - top)
    near_exp = jnp.exp(near - top)
    total = far_exp.sum(-1, keepdims=True) + near_exp.sum(-1, keepdims=True)
    far_w = (far_exp / total).astype(jnp.bfloat16).astype(jnp.float32)
    near_w = (near_exp / total).astype(jnp.bfloat16).astype(jnp.float32)
    mixed = jnp.einsum('rksgc,rckh->rskgh', far_w, values_far) + jnp.einsum('rksgj,rjkh->rskgh', near_w, values_near)
    return mixed.reshape(rows, STEPS, heads_local * HD).astype(jnp.bfloat16)

def grad_output(outputs, coef_tok, probe_part):
    sig = jax.nn.sigmoid(outputs)
    return (coef_tok[:, None] * probe_part.astype(jnp.float32)[None, :] * (sig * (1.0 + outputs * (1.0 - sig)))).astype(jnp.bfloat16)

def reference(cache_keys, cache_values, step_queries, step_keys, step_values, reward_head, lengths, assign, response_feats, out_proj, loss_probe):

    def one_row(items):
        return decode_rows(*[item[None] for item in items])[0]
    decoded = lax.map(one_row, (step_queries, cache_keys, cache_values, step_keys, step_values))
    rewards = lax.optimization_barrier(jnp.sum(decoded.astype(jnp.float32) * reward_head.astype(jnp.float32)[None, None, :], axis=(1, 2))) / STEPS
    total_rows = rewards.shape[0]
    groups = total_rows // GROUP
    group_mean = rewards.reshape(GROUP, groups).mean(0)
    advantages = rewards - jnp.tile(group_mean, GROUP)
    inverse = jnp.argsort(assign).astype(jnp.int32)
    learner_feats = response_feats[inverse]
    learner_len = lengths[inverse]
    learner_adv = advantages[inverse]
    flat_feats = learner_feats.reshape(total_rows * RESP, H * HD)
    outputs = jnp.dot(flat_feats, out_proj.T, preferred_element_type=jnp.float32)
    valid = (jnp.arange(RESP)[None, :] < learner_len[:, None]).astype(jnp.float32)
    coef = learner_adv / learner_len.astype(jnp.float32)
    coef_tok = (coef[:, None] * valid).reshape(-1)
    grad_out = grad_output(outputs, coef_tok, loss_probe)
    grad_features = jnp.dot(grad_out, out_proj, preferred_element_type=jnp.float32).astype(jnp.bfloat16)
    grad_features = grad_features.reshape(total_rows, RESP, H * HD)
    grad_proj = lax.dot_general(grad_out, flat_feats, (((0,), (0,)), ((), ())), preferred_element_type=jnp.float32)
    return (advantages, grad_features, grad_proj)
```

```python
import math

import jax
import jax.numpy as jnp
from jax import lax
from jax.sharding import Mesh
from jax.sharding import PartitionSpec as P

HD = 128
STEPS = 4
GROUP = 16
NX = 4
NY = 4
Z = ("zhi", "zlo")
S = ("zhi", "x", "zlo")
MP = ("y", "core")
BF = jnp.bfloat16
F32 = jnp.float32


def decode_rows(step_queries, cache_keys, cache_values, step_keys, step_values):
    rows = step_queries.shape[0]
    kv_local = cache_keys.shape[2] // HD
    heads_local = step_queries.shape[2] // HD
    share = heads_local // kv_local
    context = cache_keys.shape[1]
    queries = step_queries.reshape(rows, STEPS, kv_local, share, HD)
    keys_far = cache_keys.reshape(rows, context, kv_local, HD)
    values_far = cache_values.reshape(rows, context, kv_local, HD)
    keys_near = step_keys.reshape(rows, STEPS, kv_local, HD)
    values_near = step_values.reshape(rows, STEPS, kv_local, HD)
    scale = 1.0 / math.sqrt(HD)
    far = (
        jnp.einsum("rskgh,rckh->rksgc", queries, keys_far, preferred_element_type=F32)
        * scale
    )
    near = (
        jnp.einsum("rskgh,rjkh->rksgj", queries, keys_near, preferred_element_type=F32)
        * scale
    )
    causal = (jnp.arange(STEPS)[None, :] <= jnp.arange(STEPS)[:, None])[None, None, :, None, :]
    near = jnp.where(causal, near, -jnp.inf)
    top = jnp.maximum(far.max(-1), near.max(-1))[..., None]
    far_exp = jnp.exp(far - top)
    near_exp = jnp.exp(near - top)
    total = far_exp.sum(-1, keepdims=True) + near_exp.sum(-1, keepdims=True)
    far_w = (far_exp / total).astype(BF)
    near_w = (near_exp / total).astype(BF)
    mixed = jnp.einsum("rksgc,rckh->rskgh", far_w, values_far, preferred_element_type=F32)
    mixed = mixed + jnp.einsum(
        "rksgj,rjkh->rskgh", near_w, values_near, preferred_element_type=F32
    )
    return mixed.reshape(rows, STEPS, heads_local * HD).astype(BF)


def grad_output(outputs, coef_tok, probe_part):
    sig = jax.nn.sigmoid(outputs)
    return (
        coef_tok[:, None]
        * probe_part.astype(F32)[None, :]
        * (sig * (1.0 + outputs * (1.0 - sig)))
    ).astype(BF)


def shift(value, axis, size, by):
    return lax.ppermute(value, axis, [(i, (i + by) % size) for i in range(size)])


def swap(value):
    return lax.ppermute(value, "core", [(0, 1), (1, 0)])


def share_small(vector, axes):
    count = lax.axis_size(axes)
    tile = jnp.pad(vector[None, :], ((0, 7), (0, 128 - vector.shape[0])))
    copies = jnp.broadcast_to(tile[None], (count,) + tile.shape)
    got = lax.all_to_all(copies, axes, split_axis=0, concat_axis=0, tiled=True)
    return got[:, 0, : vector.shape[0]]


def dot(a, b, ca, cb, out=F32):
    return lax.dot_general(
        a, b, (((ca,), (cb,)), ((), ())), preferred_element_type=F32
    ).astype(out)


def learner(tokens, feats, weights, row_len, row_coef, probe, slots):
    per = feats.shape[0] // NX
    width = weights.shape[0]
    eighth = tokens // 8
    half = tokens // 2
    rows = row_len.shape[0]
    core = lax.axis_index("core")
    yy = lax.axis_index("y")
    ids = jnp.arange(rows)
    start = jnp.sum(jnp.where(ids[None, :] < ids[:, None], row_len[None, :], 0), 1)
    steps = jnp.arange(slots)
    place = jnp.where(
        steps[None, :] < row_len[:, None], start[:, None] + steps[None, :], -1
    ).reshape(1, -1)
    j = jnp.arange(tokens)
    owner_core = core ^ (j // half)
    owner_y = (yy + (j % half) // eighth) % NY
    q = (owner_core * NY + owner_y) * eighth + j % eighth
    pick = (q[:, None] == place).astype(BF)
    mine = q[:eighth, None]
    coef = jnp.sum(
        jnp.where(
            (start[None, :] <= mine) & (mine < (start + row_len)[None, :]),
            row_coef[None, :],
            0.0,
        ),
        1,
    )
    packed = dot(pick, feats, 1, 0, BF)
    away = swap(dot(packed[half:], weights, 1, 1, BF))
    here = dot(packed[:half], weights, 1, 1) + away.astype(F32)
    outputs = here[:eighth]
    for k in range(1, NY):
        block = here[k * eighth : (k + 1) * eighth].astype(BF)
        outputs = outputs + shift(block, "y", NY, k).astype(F32)
    grad_mine = grad_output(outputs, coef, probe)
    grad_half = jnp.concatenate(
        [grad_mine] + [shift(grad_mine, "y", NY, -k) for k in range(1, NY)], 0
    )
    grad_out = jnp.concatenate([grad_half, swap(grad_half)], 0)
    back = dot(grad_out, weights, 1, 0, BF)
    total = dot(pick[:, :per], back, 0, 0)
    for k in range(1, NX):
        part = dot(pick[:, k * per : (k + 1) * per], back, 0, 0, BF)
        total = total + shift(part, "x", NX, -k).astype(F32)
    proj = dot(grad_out, packed, 0, 0, BF)
    grad_proj = lax.psum_scatter(proj, Z, scatter_dimension=0, tiled=True).astype(F32)
    return total.astype(BF), grad_proj


def body(
    cache_keys,
    cache_values,
    step_queries,
    step_keys,
    step_values,
    reward_head,
    lengths,
    assign,
    response_feats,
    out_proj,
    loss_probe,
):
    local_rows, slots, width_local = response_feats.shape
    shards = lax.axis_size(S)
    my_shard = lax.axis_index(S)
    zhi, xx, zlo = lax.axis_index("zhi"), lax.axis_index("x"), lax.axis_index("zlo")
    weights = lax.all_gather(out_proj, Z, axis=0, tiled=True)
    own = response_feats.reshape(local_rows * slots, width_local)
    feats = jnp.concatenate([own] + [shift(own, "x", NX, k) for k in range(1, NX)], 0)

    decoded = decode_rows(step_queries, cache_keys, cache_values, step_keys, step_values)
    head_terms = jnp.dot(
        decoded.reshape(local_rows * STEPS, width_local),
        reward_head,
        preferred_element_type=F32,
    )
    head_terms = head_terms.reshape(local_rows, STEPS).sum(1) / STEPS
    row_rewards = share_small(head_terms, MP).sum(0)
    rewards = share_small(row_rewards, S).reshape(-1)
    total_rows = rewards.shape[0]
    groups = total_rows // GROUP
    group_mean = rewards.reshape(GROUP, groups).mean(0)
    advantages = rewards - jnp.tile(group_mean, GROUP)

    ids = jnp.arange(NX * local_rows)
    source = (zhi * NX + (xx - ids // local_rows) % NX) * 2 + zlo
    row = source * local_rows + ids % local_rows
    found = row[:, None] == jnp.arange(total_rows)[None, :]
    row_len = jnp.sum(jnp.where(found, lengths[None, :], 0), 1)
    row_adv = jnp.sum(jnp.where(found, advantages[None, :], 0.0), 1)
    row_coef = row_adv / row_len.astype(F32)
    per_shard = loss_probe.shape[0] // shards
    probe = lax.dynamic_index_in_dim(
        loss_probe.reshape(4, NX, 2 * per_shard), xx, 1, keepdims=False
    ).reshape(-1)

    grad_own, grad_proj = learner(
        NX * local_rows * slots, feats, weights, row_len, row_coef, probe, slots
    )

    mine = lax.dynamic_slice_in_dim(assign, my_shard * local_rows, local_rows)
    same_step = jnp.arange(slots)[:, None] == jnp.arange(slots)[None, :]
    goes = (jnp.arange(shards)[:, None] == (mine // local_rows)[None, :])
    placing = (goes[:, None, :, None] & same_step[None, :, None, :]).astype(BF)
    placing = placing.reshape(shards * slots, local_rows * slots)
    matches = assign[None, :] == (my_shard * local_rows + jnp.arange(local_rows))[:, None]
    from_shard = jnp.sum(
        jnp.where(matches, (jnp.arange(total_rows) // local_rows)[None, :], 0), 1
    )
    comes = from_shard[:, None] == jnp.arange(shards)[None, :]
    picking = (comes[:, None, :, None] & same_step[None, :, None, :]).astype(BF)
    picking = picking.reshape(local_rows * slots, shards * slots)
    outgoing = dot(placing, grad_own, 1, 0, BF)
    incoming = lax.all_to_all(outgoing, S, split_axis=0, concat_axis=0, tiled=True)
    grad_features = dot(picking, incoming, 1, 0, BF).reshape(local_rows, slots, width_local)
    return (advantages, grad_features, grad_proj)


def solution(mesh):
    fine = Mesh(
        mesh.devices.reshape(4, NX, 2, NY, 2), ("zhi", "x", "zlo", "y", "core")
    )
    rows3 = P(S, None, MP)
    placed = (
        rows3,
        rows3,
        rows3,
        rows3,
        rows3,
        P(MP),
        P(),
        P(),
        rows3,
        P(S, MP),
        P(),
    )
    return jax.shard_map(
        body,
        mesh=fine,
        in_specs=placed,
        out_specs=(P(), rows3, P(S, MP)),
        check_vma=False,
    )
```

```python
import math

import jax
import jax.numpy as jnp
from jax import lax
from jax.sharding import Mesh
from jax.sharding import PartitionSpec as P

HD = 128
STEPS = 4
GROUP = 16
NX = 4
NY = 4
Z = ("zhi", "zlo")
S = ("zhi", "x", "zlo")
MP = ("y", "core")
BF = jnp.bfloat16
F32 = jnp.float32


def decode_rows(step_queries, cache_keys, cache_values, step_keys, step_values):
    rows = step_queries.shape[0]
    kv_local = cache_keys.shape[2] // HD
    heads_local = step_queries.shape[2] // HD
    share = heads_local // kv_local
    context = cache_keys.shape[1]
    queries = step_queries.reshape(rows, STEPS, kv_local, share, HD)
    keys_far = cache_keys.reshape(rows, context, kv_local, HD)
    values_far = cache_values.reshape(rows, context, kv_local, HD)
    keys_near = step_keys.reshape(rows, STEPS, kv_local, HD)
    values_near = step_values.reshape(rows, STEPS, kv_local, HD)
    scale = 1.0 / math.sqrt(HD)
    far = (
        jnp.einsum("rskgh,rckh->rksgc", queries, keys_far, preferred_element_type=F32)
        * scale
    )
    near = (
        jnp.einsum("rskgh,rjkh->rksgj", queries, keys_near, preferred_element_type=F32)
        * scale
    )
    causal = (jnp.arange(STEPS)[None, :] <= jnp.arange(STEPS)[:, None])[None, None, :, None, :]
    near = jnp.where(causal, near, -jnp.inf)
    top = jnp.maximum(far.max(-1), near.max(-1))[..., None]
    far_exp = jnp.exp(far - top)
    near_exp = jnp.exp(near - top)
    total = far_exp.sum(-1, keepdims=True) + near_exp.sum(-1, keepdims=True)
    far_w = (far_exp / total).astype(BF)
    near_w = (near_exp / total).astype(BF)
    mixed = jnp.einsum("rksgc,rckh->rskgh", far_w, values_far, preferred_element_type=F32)
    mixed = mixed + jnp.einsum(
        "rksgj,rjkh->rskgh", near_w, values_near, preferred_element_type=F32
    )
    return mixed.reshape(rows, STEPS, heads_local * HD).astype(BF)


def grad_output(outputs, coef_tok, probe_part):
    sig = jax.nn.sigmoid(outputs)
    return (
        coef_tok[:, None]
        * probe_part.astype(F32)[None, :]
        * (sig * (1.0 + outputs * (1.0 - sig)))
    ).astype(BF)


def shift(value, axis, size, by):
    return lax.ppermute(value, axis, [(i, (i + by) % size) for i in range(size)])


def swap(value):
    return lax.ppermute(value, "core", [(0, 1), (1, 0)])


def share_small(vector, axes):
    count = lax.axis_size(axes)
    tile = jnp.pad(vector[None, :], ((0, 7), (0, 128 - vector.shape[0])))
    copies = jnp.broadcast_to(tile[None], (count,) + tile.shape)
    got = lax.all_to_all(copies, axes, split_axis=0, concat_axis=0, tiled=True)
    return got[:, 0, : vector.shape[0]]


def dot(a, b, ca, cb, out=F32):
    return lax.dot_general(
        a, b, (((ca,), (cb,)), ((), ())), preferred_element_type=F32
    ).astype(out)


def learner(tokens, blocks, weights, row_len, row_coef, probe, slots):
    per, width = blocks[0].shape
    eighth = tokens // 8
    half = tokens // 2
    rows = row_len.shape[0]
    core = lax.axis_index("core")
    yy = lax.axis_index("y")
    ids = jnp.arange(rows)
    start = jnp.sum(jnp.where(ids[None, :] < ids[:, None], row_len[None, :], 0), 1)
    steps = jnp.arange(slots)
    place = jnp.where(
        steps[None, :] < row_len[:, None], start[:, None] + steps[None, :], -1
    ).reshape(1, -1)
    j = jnp.arange(tokens)
    owner_core = core ^ (j // half)
    owner_y = (yy + (j % half) // eighth) % NY
    q = (owner_core * NY + owner_y) * eighth + j % eighth
    pick = (q[:, None] == place).astype(BF)
    mine = q[:eighth, None]
    coef = jnp.sum(
        jnp.where(
            (start[None, :] <= mine) & (mine < (start + row_len)[None, :]),
            row_coef[None, :],
            0.0,
        ),
        1,
    )
    feats = jnp.concatenate(blocks, 0)
    packed_away = dot(pick[half:], feats, 1, 0, BF)
    away = swap(dot(packed_away, weights, 1, 1, BF))
    packed_here = dot(pick[:half], feats, 1, 0, BF)
    here = dot(packed_here, weights, 1, 1) + away.astype(F32)
    outputs = here[:eighth]
    for k in range(1, NY):
        block = here[k * eighth : (k + 1) * eighth].astype(BF)
        outputs = outputs + shift(block, "y", NY, k).astype(F32)
    grad_mine = grad_output(outputs, coef, probe)
    grad_here = jnp.concatenate(
        [grad_mine] + [shift(grad_mine, "y", NY, -k) for k in range(1, NY)], 0
    )
    grad_away = swap(grad_here)
    back_here = dot(grad_here, weights, 1, 0, BF)
    proj_here = dot(grad_here, packed_here, 0, 0)
    proj = (proj_here + dot(grad_away, packed_away, 0, 0)).astype(BF)
    grad_proj = lax.psum_scatter(proj, Z, scatter_dimension=0, tiled=True).astype(F32)
    back_away = dot(grad_away, weights, 1, 0, BF)
    back = jnp.concatenate([back_here, back_away], 0)
    total = dot(pick[:, :per], back, 0, 0)
    for k in range(1, NX):
        part = dot(pick[:, k * per : (k + 1) * per], back, 0, 0, BF)
        total = total + shift(part, "x", NX, -k).astype(F32)
    return total.astype(BF), grad_proj


def body(
    cache_keys,
    cache_values,
    step_queries,
    step_keys,
    step_values,
    reward_head,
    lengths,
    assign,
    response_feats,
    out_proj,
    loss_probe,
):
    local_rows, slots, width_local = response_feats.shape
    total_rows = lengths.shape[0]
    shards = lax.axis_size(S)
    my_shard = lax.axis_index(S)
    zhi, xx, zlo = lax.axis_index("zhi"), lax.axis_index("x"), lax.axis_index("zlo")
    weights = lax.all_gather(out_proj, Z, axis=0, tiled=True)

    steps = jnp.arange(slots)
    targets = lax.dynamic_slice_in_dim(assign, my_shard * local_rows, local_rows) // local_rows
    goes = (targets[:, None] * slots + steps[None, :]).reshape(1, -1)
    placing = (jnp.arange(shards * slots)[:, None] == goes).astype(BF)
    outgoing = dot(
        placing, response_feats.reshape(local_rows * slots, width_local), 1, 0, BF
    )
    incoming = lax.all_to_all(outgoing, S, split_axis=0, concat_axis=0, tiled=True)

    decoded = decode_rows(step_queries, cache_keys, cache_values, step_keys, step_values)
    head_terms = jnp.dot(
        decoded.reshape(local_rows * STEPS, width_local),
        reward_head,
        preferred_element_type=F32,
    )
    head_terms = head_terms.reshape(local_rows, STEPS).sum(1) / STEPS
    row_rewards = share_small(head_terms, MP).sum(0)

    ids = jnp.arange(NX * local_rows)
    shard = (zhi * NX + (xx - ids // local_rows) % NX) * 2 + zlo
    slot = shard * local_rows + ids % local_rows
    found = assign[None, :] == slot[:, None]
    all_rows = jnp.arange(total_rows)
    row_len = jnp.sum(jnp.where(found, lengths[None, :], 0), 1)
    from_shard = jnp.sum(jnp.where(found[:local_rows], (all_rows // local_rows)[None, :], 0), 1)
    comes = (from_shard[:, None] * slots + steps[None, :]).reshape(-1, 1)
    picking = (comes == jnp.arange(shards * slots)[None, :]).astype(BF)
    incoming, row_rewards = lax.optimization_barrier((incoming, row_rewards))
    own = dot(picking, incoming, 1, 0, BF)
    blocks = [own] + [shift(own, "x", NX, k) for k in range(1, NX)]

    rewards = share_small(row_rewards, S).reshape(-1)
    groups = total_rows // GROUP
    group_mean = rewards.reshape(GROUP, groups).mean(0)
    advantages = rewards - jnp.tile(group_mean, GROUP)
    row_adv = jnp.sum(jnp.where(found, advantages[None, :], 0.0), 1)
    row_coef = row_adv / row_len.astype(F32)
    per_shard = loss_probe.shape[0] // shards
    probe = lax.dynamic_index_in_dim(
        loss_probe.reshape(4, NX, 2 * per_shard), xx, 1, keepdims=False
    ).reshape(-1)

    section = (assign // (NX * 2 * local_rows)) * 2 + (assign // local_rows) % 2
    loads = jnp.sum(
        jnp.where(section[None, :] == jnp.arange(8)[:, None], lengths[None, :], 0), 1
    )
    full = NX * local_rows * slots
    few = full * 2 // 3
    args = (blocks, weights, row_len, row_coef, probe)
    grad_own, grad_proj = lax.cond(
        jnp.max(loads) <= few,
        lambda a: learner(few, *a, slots),
        lambda a: learner(full, *a, slots),
        args,
    )
    grad_features = grad_own.reshape(local_rows, slots, width_local)
    return (advantages, grad_features, grad_proj)


def solution(mesh):
    fine = Mesh(
        mesh.devices.reshape(4, NX, 2, NY, 2), ("zhi", "x", "zlo", "y", "core")
    )
    rows3 = P(S, None, MP)
    placed = (
        rows3,
        rows3,
        rows3,
        rows3,
        rows3,
        P(MP),
        P(),
        P(),
        rows3,
        P(S, MP),
        P(),
    )
    return jax.shard_map(
        body,
        mesh=fine,
        in_specs=placed,
        out_specs=(P(), rows3, P(S, MP)),
        check_vma=False,
    )
```

```python
import math

import jax
import jax.numpy as jnp
from jax import lax
from jax.sharding import Mesh
from jax.sharding import PartitionSpec as P

HD = 128
STEPS = 4
GROUP = 16
NX = 4
NY = 4
Z = ("zhi", "zlo")
S = ("zhi", "x", "zlo")
MP = ("y", "core")
BF = jnp.bfloat16
F32 = jnp.float32


def decode_rows(step_queries, cache_keys, cache_values, step_keys, step_values):
    rows = step_queries.shape[0]
    kv_local = cache_keys.shape[2] // HD
    heads_local = step_queries.shape[2] // HD
    share = heads_local // kv_local
    context = cache_keys.shape[1]
    queries = step_queries.reshape(rows, STEPS, kv_local, share, HD)
    keys_far = cache_keys.reshape(rows, context, kv_local, HD)
    values_far = cache_values.reshape(rows, context, kv_local, HD)
    keys_near = step_keys.reshape(rows, STEPS, kv_local, HD)
    values_near = step_values.reshape(rows, STEPS, kv_local, HD)
    scale = 1.0 / math.sqrt(HD)
    far = (
        jnp.einsum("rskgh,rckh->rksgc", queries, keys_far, preferred_element_type=F32)
        * scale
    )
    near = (
        jnp.einsum("rskgh,rjkh->rksgj", queries, keys_near, preferred_element_type=F32)
        * scale
    )
    causal = (jnp.arange(STEPS)[None, :] <= jnp.arange(STEPS)[:, None])[None, None, :, None, :]
    near = jnp.where(causal, near, -jnp.inf)
    top = jnp.maximum(far.max(-1), near.max(-1))[..., None]
    far_exp = jnp.exp(far - top)
    near_exp = jnp.exp(near - top)
    total = far_exp.sum(-1, keepdims=True) + near_exp.sum(-1, keepdims=True)
    far_w = (far_exp / total).astype(BF)
    near_w = (near_exp / total).astype(BF)
    mixed = jnp.einsum("rksgc,rckh->rskgh", far_w, values_far, preferred_element_type=F32)
    mixed = mixed + jnp.einsum(
        "rksgj,rjkh->rskgh", near_w, values_near, preferred_element_type=F32
    )
    return mixed.reshape(rows, STEPS, heads_local * HD).astype(BF)


def grad_output(outputs, coef_tok, probe_part):
    sig = jax.nn.sigmoid(outputs)
    return (
        coef_tok[:, None]
        * probe_part.astype(F32)[None, :]
        * (sig * (1.0 + outputs * (1.0 - sig)))
    ).astype(BF)


def shift(value, axis, size, by):
    return lax.ppermute(value, axis, [(i, (i + by) % size) for i in range(size)])


def swap(value):
    return lax.ppermute(value, "core", [(0, 1), (1, 0)])


def share_small(vector, axes):
    count = lax.axis_size(axes)
    tile = jnp.pad(vector[None, :], ((0, 7), (0, 128 - vector.shape[0])))
    copies = jnp.broadcast_to(tile[None], (count,) + tile.shape)
    got = lax.all_to_all(copies, axes, split_axis=0, concat_axis=0, tiled=True)
    return got[:, 0, : vector.shape[0]]


def dot(a, b, ca, cb, out=F32):
    return lax.dot_general(
        a, b, (((ca,), (cb,)), ((), ())), preferred_element_type=F32
    ).astype(out)


def section_plan(tokens, per, slots, row_len, low, high):
    start = row_len.reshape(NX, -1)
    count = start.shape[1]
    ids = jnp.arange(count)
    before = ids[None, None, :] < ids[None, :, None]
    start = jnp.sum(jnp.where(before, start[:, None, :], 0), 2)
    blocks = jnp.arange(NX)
    base = jnp.sum(
        jnp.where(blocks[None, :] < blocks[:, None], (high - low)[None, :], 0), 1
    )
    spot = jnp.arange(per)[None, :]
    place = jnp.where(
        (spot >= low[:, None]) & (spot < high[:, None]), (base - low)[:, None] + spot, -1
    ).reshape(-1)
    ends = jnp.minimum(start + row_len.reshape(NX, -1), high[:, None])
    first = jnp.maximum(start, low[:, None])
    run_start = ((base - low)[:, None] + first).reshape(-1)
    run_end = run_start + jnp.maximum(ends - first, 0).reshape(-1)
    half = tokens // 2
    eighth = tokens // 8
    j = jnp.arange(tokens)
    owner_core = lax.axis_index("core") ^ (j // half)
    owner_y = (lax.axis_index("y") + (j % half) // eighth) % NY
    q = (owner_core * NY + owner_y) * eighth + j % eighth
    pick = (q[:, None] == place[None, :]).astype(BF)
    unpick = (place[:, None] == q[None, :]).astype(BF)
    mine = q[:eighth, None]
    rows_of = (run_start[None, :] <= mine) & (mine < run_end[None, :])
    return pick, unpick, rows_of


def gather_x(own):
    return jnp.concatenate([own] + [shift(own, "x", NX, k) for k in range(1, NX)], 0)


def forward(tokens, feats, weights, pick):
    half = tokens // 2
    packed_away = dot(pick[half:], feats, 1, 0, BF)
    away = swap(dot(packed_away, weights, 1, 1, BF))
    packed_here = dot(pick[:half], feats, 1, 0, BF)
    here = dot(packed_here, weights, 1, 1) + away.astype(F32)
    return here, packed_here, packed_away


def sum_y(here):
    eighth = here.shape[0] // NY
    outputs = here[:eighth]
    for k in range(1, NY):
        block = here[k * eighth : (k + 1) * eighth].astype(BF)
        outputs = outputs + shift(block, "y", NY, k).astype(F32)
    return outputs


def backward(grad_mine, packed_here, packed_away, weights, unpick):
    parts = [grad_mine] + [shift(grad_mine, "y", NY, -k) for k in range(1, NY)]
    grad_here = jnp.concatenate(parts, 0)
    grad_away = jnp.concatenate([swap(part) for part in parts], 0)
    proj = dot(grad_here, packed_here, 0, 0) + dot(grad_away, packed_away, 0, 0)
    grad_proj = lax.psum_scatter(proj.astype(BF), Z, scatter_dimension=0, tiled=True)
    back = jnp.concatenate(
        [dot(grad_here, weights, 1, 0, BF), dot(grad_away, weights, 1, 0, BF)], 0
    )
    per = unpick.shape[0] // NX
    total = dot(unpick[:per], back, 1, 0)
    for k in range(1, NX):
        part = dot(unpick[k * per : (k + 1) * per], back, 1, 0, BF)
        total = total + shift(part, "x", NX, -k).astype(F32)
    return total.astype(BF), grad_proj.astype(F32)


def body(
    cache_keys,
    cache_values,
    step_queries,
    step_keys,
    step_values,
    reward_head,
    lengths,
    assign,
    response_feats,
    out_proj,
    loss_probe,
):
    local_rows, slots, width_local = response_feats.shape
    total_rows = lengths.shape[0]
    shards = lax.axis_size(S)
    my_shard = lax.axis_index(S)
    zhi, xx, zlo = lax.axis_index("zhi"), lax.axis_index("x"), lax.axis_index("zlo")
    full = local_rows * slots
    few = 304
    section_full = NX * full
    section_few = 1024
    weights = lax.all_gather(out_proj, Z, axis=0, tiled=True)

    steps = jnp.arange(slots)
    targets = lax.dynamic_slice_in_dim(assign, my_shard * local_rows, local_rows) // local_rows
    goes = (targets[:, None] * slots + steps[None, :]).reshape(1, -1)
    placing = (jnp.arange(shards * slots)[:, None] == goes).astype(BF)
    outgoing = dot(placing, response_feats.reshape(full, width_local), 1, 0, BF)
    step_queries, outgoing = lax.optimization_barrier((step_queries, outgoing))
    incoming = lax.all_to_all(outgoing, S, split_axis=0, concat_axis=0, tiled=True)

    decoded = decode_rows(step_queries, cache_keys, cache_values, step_keys, step_values)
    head_terms = jnp.dot(
        decoded.reshape(local_rows * STEPS, width_local),
        reward_head,
        preferred_element_type=F32,
    )
    head_terms = head_terms.reshape(local_rows, STEPS).sum(1) / STEPS

    ids = jnp.arange(NX * local_rows)
    shard = (zhi * NX + (xx - ids // local_rows) % NX) * 2 + zlo
    slot = shard * local_rows + ids % local_rows
    found = assign[None, :] == slot[:, None]
    all_rows = jnp.arange(total_rows)
    row_len = jnp.sum(jnp.where(found, lengths[None, :], 0), 1)
    from_shard = jnp.sum(jnp.where(found[:local_rows], (all_rows // local_rows)[None, :], 0), 1)
    own_len = row_len[:local_rows]
    own_ids = jnp.arange(local_rows)
    own_start = jnp.sum(
        jnp.where(own_ids[None, :] < own_ids[:, None], own_len[None, :], 0), 1
    )
    comes = from_shard[None, :] == jnp.arange(shards)[:, None]
    src_start = jnp.sum(jnp.where(comes, own_start[None, :], 0), 1)
    src_len = jnp.sum(jnp.where(comes, own_len[None, :], 0), 1)
    lies = jnp.where(
        steps[None, :] < src_len[:, None], src_start[:, None] + steps[None, :], -1
    ).reshape(1, -1)
    wants = jnp.where(
        steps[None, :] < own_len[:, None], own_start[:, None] + steps[None, :], -1
    ).reshape(-1, 1)
    picking = (jnp.arange(few)[:, None] == lies).astype(BF)
    leaving = (wants == jnp.arange(few)[None, :]).astype(BF)

    shard_len = jnp.sum(row_len.reshape(NX, local_rows), 1)
    capped = jnp.minimum(shard_len, few)
    blocks = jnp.arange(NX)
    ahead = jnp.sum(jnp.where(blocks[None, :] < blocks[:, None], capped[None, :], 0), 1)
    taken = jnp.clip(section_few - ahead, 0, capped)
    pick, unpick, rows_of = section_plan(
        section_few, few, slots, row_len, jnp.zeros_like(taken), taken
    )
    pick, unpick, picking, leaving, incoming, head_terms = lax.optimization_barrier(
        (pick, unpick, picking, leaving, incoming, head_terms)
    )
    own = dot(picking, incoming, 1, 0, BF)
    own, head_terms = lax.optimization_barrier((own, head_terms))
    row_rewards = share_small(head_terms, MP).sum(0)
    feats, row_rewards = lax.optimization_barrier((gather_x(own), row_rewards))
    here, packed_here, packed_away = forward(section_few, feats, weights, pick)

    here, row_rewards = lax.optimization_barrier((here, row_rewards))
    rewards = share_small(row_rewards, S).reshape(-1)
    groups = total_rows // GROUP
    group_mean = rewards.reshape(GROUP, groups).mean(0)
    advantages = rewards - jnp.tile(group_mean, GROUP)
    row_adv = jnp.sum(jnp.where(found, advantages[None, :], 0.0), 1)
    row_coef = row_adv / row_len.astype(F32)
    per_shard = loss_probe.shape[0] // shards
    probe = lax.dynamic_index_in_dim(
        loss_probe.reshape(4, NX, 2 * per_shard), xx, 1, keepdims=False
    ).reshape(-1)

    coef = jnp.sum(jnp.where(rows_of, row_coef[None, :], 0.0), 1)
    grad_mine = grad_output(sum_y(here), coef, probe)
    total, grad_proj = backward(grad_mine, packed_here, packed_away, weights, unpick)
    grad_own = dot(leaving, total, 1, 0, BF)

    loads = jnp.sum(
        jnp.where(
            (assign // local_rows)[None, :] == jnp.arange(shards)[:, None], lengths[None, :], 0
        ),
        1,
    )
    sections = loads.reshape(4, NX, 2).sum(1)
    more = (jnp.max(loads) > few) | (jnp.max(sections) > section_few)

    def rest(args):
        grad_own, grad_proj, incoming, weights, row_coef, probe, lies, wants = args
        rest_tokens = section_full - section_few
        pick, unpick, rows_of = section_plan(
            rest_tokens, full, slots, row_len, taken, shard_len
        )
        picking = (jnp.arange(full)[:, None] == lies).astype(BF)
        leaving = (wants == jnp.arange(full)[None, :]).astype(BF)
        feats = gather_x(dot(picking, incoming, 1, 0, BF))
        here, packed_here, packed_away = forward(rest_tokens, feats, weights, pick)
        coef = jnp.sum(jnp.where(rows_of, row_coef[None, :], 0.0), 1)
        grad_mine = grad_output(sum_y(here), coef, probe)
        total, proj = backward(grad_mine, packed_here, packed_away, weights, unpick)
        return grad_own + dot(leaving, total, 1, 0, BF), grad_proj + proj

    grad_own, grad_proj = lax.cond(
        more,
        rest,
        lambda args: (args[0], args[1]),
        (grad_own, grad_proj, incoming, weights, row_coef, probe, lies, wants),
    )
    grad_features = grad_own.reshape(local_rows, slots, width_local)
    return (advantages, grad_features, grad_proj)


def solution(mesh):
    fine = Mesh(
        mesh.devices.reshape(4, NX, 2, NY, 2), ("zhi", "x", "zlo", "y", "core")
    )
    rows3 = P(S, None, MP)
    placed = (
        rows3,
        rows3,
        rows3,
        rows3,
        rows3,
        P(MP),
        P(),
        P(),
        rows3,
        P(S, MP),
        P(),
    )
    return jax.shard_map(
        body,
        mesh=fine,
        in_specs=placed,
        out_specs=(P(), rows3, P(S, MP)),
        check_vma=False,
    )
```

```python
import math

import jax
import jax.numpy as jnp
from jax import lax
from jax.sharding import Mesh
from jax.sharding import PartitionSpec as P

HD = 128
STEPS = 4
GROUP = 16
NX = 4
NY = 4
Z = ("zhi", "zlo")
S = ("zhi", "x", "zlo")
MP = ("y", "core")
BF = jnp.bfloat16
F32 = jnp.float32


def decode_rows(step_queries, cache_keys, cache_values, step_keys, step_values):
    rows = step_queries.shape[0]
    kv_local = cache_keys.shape[2] // HD
    heads_local = step_queries.shape[2] // HD
    share = heads_local // kv_local
    context = cache_keys.shape[1]
    queries = step_queries.reshape(rows, STEPS, kv_local, share, HD)
    keys_far = cache_keys.reshape(rows, context, kv_local, HD)
    values_far = cache_values.reshape(rows, context, kv_local, HD)
    keys_near = step_keys.reshape(rows, STEPS, kv_local, HD)
    values_near = step_values.reshape(rows, STEPS, kv_local, HD)
    scale = 1.0 / math.sqrt(HD)
    far = (
        jnp.einsum("rskgh,rckh->rksgc", queries, keys_far, preferred_element_type=F32)
        * scale
    )
    near = (
        jnp.einsum("rskgh,rjkh->rksgj", queries, keys_near, preferred_element_type=F32)
        * scale
    )
    causal = (jnp.arange(STEPS)[None, :] <= jnp.arange(STEPS)[:, None])[None, None, :, None, :]
    near = jnp.where(causal, near, -jnp.inf)
    top = jnp.maximum(far.max(-1), near.max(-1))[..., None]
    far_exp = jnp.exp(far - top)
    near_exp = jnp.exp(near - top)
    total = far_exp.sum(-1, keepdims=True) + near_exp.sum(-1, keepdims=True)
    far_w = (far_exp / total).astype(BF)
    near_w = (near_exp / total).astype(BF)
    mixed = jnp.einsum("rksgc,rckh->rskgh", far_w, values_far, preferred_element_type=F32)
    mixed = mixed + jnp.einsum(
        "rksgj,rjkh->rskgh", near_w, values_near, preferred_element_type=F32
    )
    return mixed.reshape(rows, STEPS, heads_local * HD).astype(BF)


def grad_output(outputs, coef_tok, probe_part):
    sig = jax.nn.sigmoid(outputs)
    return (
        coef_tok[:, None]
        * probe_part.astype(F32)[None, :]
        * (sig * (1.0 + outputs * (1.0 - sig)))
    ).astype(BF)


def shift(value, axis, size, by):
    return lax.ppermute(value, axis, [(i, (i + by) % size) for i in range(size)])


def swap(value):
    return lax.ppermute(value, "core", [(0, 1), (1, 0)])


def after(value, earlier):
    return lax.optimization_barrier((value, earlier))[0]


def sum_mp(vector):
    tile = jnp.pad(vector[None, :], ((0, 7), (0, 128 - vector.shape[0])))
    tile = tile + swap(tile)
    near = shift(tile, "y", NY, 1) + shift(tile, "y", NY, 3)
    return ((tile + shift(tile, "y", NY, 2)) + near)[0, : vector.shape[0]]


def dot(a, b, ca, cb, out=F32):
    return lax.dot_general(
        a, b, (((ca,), (cb,)), ((), ())), preferred_element_type=F32
    ).astype(out)


def section_plan(tokens, per, spans, live, low, high):
    spans = spans.reshape(NX, -1)
    count = spans.shape[1]
    ids = jnp.arange(count)
    before = ids[None, None, :] < ids[None, :, None]
    start = jnp.sum(jnp.where(before, spans[:, None, :], 0), 2)
    blocks = jnp.arange(NX)
    base = jnp.sum(
        jnp.where(blocks[None, :] < blocks[:, None], (high - low)[None, :], 0), 1
    )
    spot = jnp.arange(per)[None, :]
    place = jnp.where(
        (spot >= low[:, None]) & (spot < high[:, None]), (base - low)[:, None] + spot, -1
    ).reshape(-1)
    ends = jnp.minimum(start + live.reshape(NX, -1), high[:, None])
    first = jnp.maximum(start, low[:, None])
    run_start = ((base - low)[:, None] + first).reshape(-1)
    run_end = run_start + jnp.maximum(ends - first, 0).reshape(-1)
    half = tokens // 2
    eighth = tokens // 8
    j = jnp.arange(tokens)
    owner_core = lax.axis_index("core") ^ (j // half)
    owner_y = (lax.axis_index("y") + (j % half) // eighth) % NY
    q = (owner_core * NY + owner_y) * eighth + j % eighth
    pick = (q[:, None] == place[None, :]).astype(BF)
    unpick = (place[:, None] == q[None, :]).astype(BF)
    mine = q[:eighth, None]
    rows_of = (run_start[None, :] <= mine) & (mine < run_end[None, :])
    return pick, unpick, rows_of


def gather_x(own):
    parts = [own] + [shift(own, "x", NX, k) for k in range(1, NX)]
    return jnp.concatenate(parts, 0), parts[1]


def forward(tokens, feats, weights, pick):
    half = tokens // 2
    packed_away = dot(pick[half:], feats, 1, 0, BF)
    away = swap(dot(packed_away, weights, 1, 1, BF))
    packed_here = dot(pick[:half], feats, 1, 0, BF)
    here = dot(packed_here, weights, 1, 1) + away.astype(F32)
    return here, packed_here, packed_away


def sum_y(here):
    eighth = here.shape[0] // NY
    outputs = here[:eighth]
    parts = []
    for k in range(1, NY):
        block = here[k * eighth : (k + 1) * eighth].astype(BF)
        parts.append(shift(block, "y", NY, k))
        outputs = outputs + parts[-1].astype(F32)
    return outputs, parts[0]


def gather_y(grad_mine, pieces):
    parts = [grad_mine] + [shift(grad_mine, "y", NY, -k) for k in range(1, NY)]
    grad_here = jnp.concatenate(parts, 0)
    if pieces:
        grad_away = jnp.concatenate([swap(part) for part in parts], 0)
    else:
        grad_away = swap(grad_here)
    return grad_here, grad_away


def proj_terms(grad_here, grad_away, packed_here, packed_away):
    return dot(grad_here, packed_here, 0, 0) + dot(grad_away, packed_away, 0, 0)


def sum_z(proj):
    return lax.psum_scatter(proj, Z, scatter_dimension=0, tiled=True)


def feature_grad(grad_here, grad_away, weights, unpick):
    back = jnp.concatenate(
        [dot(grad_here, weights, 1, 0, BF), dot(grad_away, weights, 1, 0, BF)], 0
    )
    per = unpick.shape[0] // NX
    total = dot(unpick[:per], back, 1, 0)
    for k in range(1, NX):
        part = dot(unpick[k * per : (k + 1) * per], back, 1, 0, BF)
        total = total + shift(part, "x", NX, -k).astype(F32)
    return total.astype(BF)


def body(
    cache_keys,
    cache_values,
    step_queries,
    step_keys,
    step_values,
    reward_head,
    lengths,
    assign,
    response_feats,
    out_proj,
    loss_probe,
):
    local_rows, slots, width_local = response_feats.shape
    total_rows = lengths.shape[0]
    shards = lax.axis_size(S)
    my_shard = lax.axis_index(S)
    zhi, xx, zlo = lax.axis_index("zhi"), lax.axis_index("x"), lax.axis_index("zlo")
    head = 16
    tail = slots - head
    full = local_rows * slots
    head_shard = local_rows * head
    head_section = NX * head_shard
    tail_shard = local_rows * tail
    tail_section = NX * tail_shard
    few_shard = 96
    few_section = 256
    weights = lax.all_gather(out_proj, Z, axis=0, tiled=True)

    own_feats = response_feats.reshape(full, width_local)
    targets = lax.dynamic_slice_in_dim(assign, my_shard * local_rows, local_rows) // local_rows
    steps = jnp.arange(slots)[None, :]
    goes_head = jnp.where(steps < head, targets[:, None] * head + steps, -1)
    goes_tail = jnp.where(steps >= head, targets[:, None] * head + steps - head, -1)
    block_rows = jnp.arange(shards * head)[:, None]
    placing_head = (block_rows == goes_head.reshape(1, -1)).astype(BF)
    outgoing_head = dot(placing_head, own_feats, 1, 0, BF)
    step_queries, outgoing_head, own_feats = lax.optimization_barrier(
        (step_queries, outgoing_head, own_feats)
    )
    incoming_head = lax.all_to_all(outgoing_head, S, split_axis=0, concat_axis=0, tiled=True)

    decoded = decode_rows(step_queries, cache_keys, cache_values, step_keys, step_values)
    head_terms = jnp.dot(
        decoded.reshape(local_rows * STEPS, width_local),
        reward_head,
        preferred_element_type=F32,
    )
    row_rewards = sum_mp(head_terms.reshape(local_rows, STEPS).sum(1) / STEPS)
    high = row_rewards.astype(BF).astype(F32)
    middle = (row_rewards - high).astype(BF).astype(F32)
    low = row_rewards - high - middle
    terms = jnp.concatenate([high, middle, low])
    terms = jnp.pad(terms, (0, width_local - terms.shape[0]))
    placing_tail = (block_rows == goes_tail.reshape(1, -1)).astype(BF)
    outgoing_tail = dot(placing_tail, own_feats, 1, 0)
    outgoing_tail = jnp.where(block_rows % head == tail, terms[None, :], outgoing_tail).astype(BF)

    ids = jnp.arange(NX * local_rows)
    shard = (zhi * NX + (xx - ids // local_rows) % NX) * 2 + zlo
    slot = shard * local_rows + ids % local_rows
    found = assign[None, :] == slot[:, None]
    all_rows = jnp.arange(total_rows)
    row_len = jnp.sum(jnp.where(found, lengths[None, :], 0), 1)
    from_shard = jnp.sum(jnp.where(found[:local_rows], (all_rows // local_rows)[None, :], 0), 1)
    head_len = jnp.minimum(row_len, head)
    tail_len = row_len - head_len
    own_tail = tail_len[:local_rows]
    own_ids = jnp.arange(local_rows)
    own_start = jnp.sum(
        jnp.where(own_ids[None, :] < own_ids[:, None], own_tail[None, :], 0), 1
    )
    head_steps = jnp.arange(head)[None, :]
    comes_head = (from_shard[:, None] * head + head_steps).reshape(-1, 1)
    picking_head = (comes_head == jnp.arange(shards * head)[None, :]).astype(BF)
    comes = from_shard[None, :] == jnp.arange(shards)[:, None]
    src_start = jnp.sum(jnp.where(comes, own_start[None, :], 0), 1)
    src_tail = jnp.sum(jnp.where(comes, own_tail[None, :], 0), 1)
    lies = jnp.where(head_steps < src_tail[:, None], src_start[:, None] + head_steps, -1)
    lies = lies.reshape(1, -1)
    picking_tail = (jnp.arange(few_shard)[:, None] == lies).astype(BF)
    wants_head = jnp.where(steps < head, own_ids[:, None] * head + steps, -1).reshape(-1, 1)
    wants_tail = jnp.where(
        (steps >= head) & (steps - head < own_tail[:, None]),
        own_start[:, None] + steps - head,
        -1,
    ).reshape(-1, 1)
    leaving_head = (wants_head == jnp.arange(head_shard)[None, :]).astype(BF)
    leaving_tail = (wants_tail == jnp.arange(few_shard)[None, :]).astype(BF)

    shard_tail = jnp.sum(tail_len.reshape(NX, local_rows), 1)
    capped = jnp.minimum(shard_tail, few_shard)
    blocks = jnp.arange(NX)
    ahead = jnp.sum(jnp.where(blocks[None, :] < blocks[:, None], capped[None, :], 0), 1)
    taken = jnp.clip(few_section - ahead, 0, capped)
    none = jnp.zeros_like(taken)
    pick_h, unpick_h, rows_h = section_plan(
        head_section, head_shard, jnp.full_like(row_len, head), head_len, none, none + head_shard
    )
    pick_t, unpick_t, rows_t = section_plan(
        few_section, few_shard, tail_len, tail_len, none, taken
    )
    masks = (pick_h, unpick_h, pick_t, unpick_t, picking_head, picking_tail)
    masks = masks + (leaving_head, leaving_tail)
    masks, incoming_head, outgoing_tail = lax.optimization_barrier(
        (masks, incoming_head, outgoing_tail)
    )
    pick_h, unpick_h, pick_t, unpick_t, picking_head, picking_tail = masks[:6]
    leaving_head, leaving_tail = masks[6:]
    feats_h, first_h = gather_x(dot(picking_head, incoming_head, 1, 0, BF))
    outgoing_tail = after(outgoing_tail, first_h)
    incoming_tail = lax.all_to_all(outgoing_tail, S, split_axis=0, concat_axis=0, tiled=True)

    terms = incoming_tail.reshape(shards, head, width_local)[:, tail, : 3 * local_rows]
    terms = terms.astype(F32)
    rewards = terms[:, :local_rows] + terms[:, local_rows : 2 * local_rows]
    rewards = (rewards + terms[:, 2 * local_rows :]).reshape(-1)
    groups = total_rows // GROUP
    group_mean = rewards.reshape(GROUP, groups).mean(0)
    advantages = rewards - jnp.tile(group_mean, GROUP)
    row_adv = jnp.sum(jnp.where(found, advantages[None, :], 0.0), 1)
    row_coef = row_adv / row_len.astype(F32)
    per_shard = loss_probe.shape[0] // shards
    probe = lax.dynamic_index_in_dim(
        loss_probe.reshape(4, NX, 2 * per_shard), xx, 1, keepdims=False
    ).reshape(-1)

    def gradient(here, rows_of):
        coef = jnp.sum(jnp.where(rows_of, row_coef[None, :], 0.0), 1)
        outputs, first = sum_y(here)
        return grad_output(outputs, coef, probe), first

    here_h, packed_hh, packed_ha = forward(head_section, feats_h, weights, pick_h)
    grad_h, first_h = gradient(here_h, rows_h)
    own_t = after(dot(picking_tail, incoming_tail, 1, 0, BF), first_h)
    feats_t = after(gather_x(own_t)[0], grad_h)
    grad_hh, grad_ha = gather_y(grad_h, True)
    here_t, packed_th, packed_ta = forward(few_section, feats_t, weights, pick_t)
    grad_th, grad_ta = gather_y(gradient(here_t, rows_t)[0], False)
    proj = proj_terms(grad_hh, grad_ha, packed_hh, packed_ha)
    proj = proj + proj_terms(grad_th, grad_ta, packed_th, packed_ta)
    proj = proj.astype(BF)
    grad_proj = sum_z(proj).astype(F32)
    grad_th = after(grad_th, proj)
    total_h = feature_grad(grad_hh, grad_ha, weights, unpick_h)
    total_t = feature_grad(grad_th, grad_ta, weights, unpick_t)
    grad_own = dot(leaving_head, total_h, 1, 0) + dot(leaving_tail, total_t, 1, 0)
    grad_own = grad_own.astype(BF)

    tails = jnp.maximum(lengths - head, 0)
    loads = jnp.sum(
        jnp.where(
            (assign // local_rows)[None, :] == jnp.arange(shards)[:, None], tails[None, :], 0
        ),
        1,
    )
    sections = loads.reshape(4, NX, 2).sum(1)
    more = (jnp.max(loads) > few_shard) | (jnp.max(sections) > few_section)

    def rest(args):
        grad_own, grad_proj, incoming_tail, weights, lies, wants = args
        rest_section = tail_section - few_section
        pick, unpick, rows_of = section_plan(
            rest_section, tail_shard, tail_len, tail_len, taken, shard_tail
        )
        picking = (jnp.arange(tail_shard)[:, None] == lies).astype(BF)
        leaving = (wants == jnp.arange(tail_shard)[None, :]).astype(BF)
        feats = gather_x(dot(picking, incoming_tail, 1, 0, BF))[0]
        here, packed_here, packed_away = forward(rest_section, feats, weights, pick)
        grad_here, grad_away = gather_y(gradient(here, rows_of)[0], False)
        proj = proj_terms(grad_here, grad_away, packed_here, packed_away)
        proj = sum_z(proj.astype(BF))
        total = feature_grad(grad_here, grad_away, weights, unpick)
        return grad_own + dot(leaving, total, 1, 0, BF), grad_proj + proj.astype(F32)

    grad_own, grad_proj = lax.cond(
        more,
        rest,
        lambda args: (args[0], args[1]),
        (grad_own, grad_proj, incoming_tail, weights, lies, wants_tail),
    )
    grad_features = grad_own.reshape(local_rows, slots, width_local)
    return (advantages, grad_features, grad_proj)


def solution(mesh):
    fine = Mesh(
        mesh.devices.reshape(4, NX, 2, NY, 2), ("zhi", "x", "zlo", "y", "core")
    )
    rows3 = P(S, None, MP)
    placed = (
        rows3,
        rows3,
        rows3,
        rows3,
        rows3,
        P(MP),
        P(),
        P(),
        rows3,
        P(S, MP),
        P(),
    )
    return jax.shard_map(
        body,
        mesh=fine,
        in_specs=placed,
        out_specs=(P(), rows3, P(S, MP)),
        check_vma=False,
    )
```

```python
import math

import jax
import jax.numpy as jnp
from jax import lax
from jax.sharding import Mesh
from jax.sharding import PartitionSpec as P

HD = 128
STEPS = 4
GROUP = 16
NX = 4
NY = 4
Z = ("zhi", "zlo")
S = ("zhi", "x", "zlo")
MP = ("y", "core")
BF = jnp.bfloat16
F32 = jnp.float32


def decode_rows(step_queries, cache_keys, cache_values, step_keys, step_values):
    rows = step_queries.shape[0]
    kv_local = cache_keys.shape[2] // HD
    heads_local = step_queries.shape[2] // HD
    share = heads_local // kv_local
    context = cache_keys.shape[1]
    queries = step_queries.reshape(rows, STEPS, kv_local, share, HD)
    keys_far = cache_keys.reshape(rows, context, kv_local, HD)
    values_far = cache_values.reshape(rows, context, kv_local, HD)
    keys_near = step_keys.reshape(rows, STEPS, kv_local, HD)
    values_near = step_values.reshape(rows, STEPS, kv_local, HD)
    scale = 1.0 / math.sqrt(HD)
    far = (
        jnp.einsum("rskgh,rckh->rksgc", queries, keys_far, preferred_element_type=F32)
        * scale
    )
    near = (
        jnp.einsum("rskgh,rjkh->rksgj", queries, keys_near, preferred_element_type=F32)
        * scale
    )
    causal = (jnp.arange(STEPS)[None, :] <= jnp.arange(STEPS)[:, None])[None, None, :, None, :]
    near = jnp.where(causal, near, -jnp.inf)
    top = jnp.maximum(far.max(-1), near.max(-1))[..., None]
    far_exp = jnp.exp(far - top)
    near_exp = jnp.exp(near - top)
    total = far_exp.sum(-1, keepdims=True) + near_exp.sum(-1, keepdims=True)
    far_w = (far_exp / total).astype(BF)
    near_w = (near_exp / total).astype(BF)
    mixed = jnp.einsum("rksgc,rckh->rskgh", far_w, values_far, preferred_element_type=F32)
    mixed = mixed + jnp.einsum(
        "rksgj,rjkh->rskgh", near_w, values_near, preferred_element_type=F32
    )
    return mixed.reshape(rows, STEPS, heads_local * HD).astype(BF)


def grad_output(outputs, coef_tok, probe_part):
    sig = jax.nn.sigmoid(outputs)
    return (
        coef_tok[:, None]
        * probe_part.astype(F32)[None, :]
        * (sig * (1.0 + outputs * (1.0 - sig)))
    ).astype(BF)


def shift(value, axis, size, by):
    return lax.ppermute(value, axis, [(i, (i + by) % size) for i in range(size)])


def swap(value):
    return lax.ppermute(value, "core", [(0, 1), (1, 0)])


def share_small(vector, axes):
    count = lax.axis_size(axes)
    tile = jnp.pad(vector[None, :], ((0, 7), (0, 128 - vector.shape[0])))
    copies = jnp.broadcast_to(tile[None], (count,) + tile.shape)
    got = lax.all_to_all(copies, axes, split_axis=0, concat_axis=0, tiled=True)
    return got[:, 0, : vector.shape[0]]


def after(value, earlier):
    return lax.optimization_barrier((value, earlier))[0]


def sum_mp(vector):
    tile = jnp.pad(vector[None, :], ((0, 7), (0, 128 - vector.shape[0])))
    tile = tile + swap(tile)
    near = shift(tile, "y", NY, 1) + shift(tile, "y", NY, 3)
    return ((tile + shift(tile, "y", NY, 2)) + near)[0, : vector.shape[0]]


def dot(a, b, ca, cb, out=F32):
    return lax.dot_general(
        a, b, (((ca,), (cb,)), ((), ())), preferred_element_type=F32
    ).astype(out)


def section_plan(tokens, per, slots, row_len, low, high):
    start = row_len.reshape(NX, -1)
    count = start.shape[1]
    ids = jnp.arange(count)
    before = ids[None, None, :] < ids[None, :, None]
    start = jnp.sum(jnp.where(before, start[:, None, :], 0), 2)
    blocks = jnp.arange(NX)
    base = jnp.sum(
        jnp.where(blocks[None, :] < blocks[:, None], (high - low)[None, :], 0), 1
    )
    spot = jnp.arange(per)[None, :]
    place = jnp.where(
        (spot >= low[:, None]) & (spot < high[:, None]), (base - low)[:, None] + spot, -1
    )
    ends = jnp.minimum(start + row_len.reshape(NX, -1), high[:, None])
    first = jnp.maximum(start, low[:, None])
    run_start = ((base - low)[:, None] + first).reshape(-1)
    run_end = run_start + jnp.maximum(ends - first, 0).reshape(-1)
    half = tokens // 2
    eighth = tokens // 8
    j = jnp.arange(tokens)
    owner_core = lax.axis_index("core") ^ (j // half)
    owner_y = (lax.axis_index("y") + (j % half) // eighth) % NY
    q = (owner_core * NY + owner_y) * eighth + j % eighth
    pick = [(q[:, None] == place[k][None, :]).astype(BF) for k in range(NX)]
    unpick = [(place[k][:, None] == q[None, :]).astype(BF) for k in range(NX)]
    mine = q[:eighth, None]
    rows_of = (run_start[None, :] <= mine) & (mine < run_end[None, :])
    return pick, unpick, rows_of


def gather_x(own):
    return [own] + [shift(own, "x", NX, k) for k in range(1, NX)]


ARRIVE = (0, 1, 3, 2)


def forward(feats, weights, pick):
    packed = sum(dot(pick[k], feats[k], 1, 0) for k in ARRIVE).astype(BF)
    half = packed.shape[0] // 2
    away = swap(dot(packed[half:], weights, 1, 1, BF))
    here = dot(packed[:half], weights, 1, 1) + away.astype(F32)
    return here, packed


def sum_y(here):
    eighth = here.shape[0] // NY
    outputs = here[:eighth]
    for k in range(1, NY):
        block = here[k * eighth : (k + 1) * eighth].astype(BF)
        outputs = outputs + shift(block, "y", NY, k).astype(F32)
    return outputs


def backward(grad_mine, packed, weights, unpick):
    near = [grad_mine] + [shift(grad_mine, "y", NY, -k) for k in range(1, NY)]
    far = [swap(part) for part in near]
    eighth = grad_mine.shape[0]
    proj = 0.0
    for k in ARRIVE:
        mine = packed[k * eighth : (k + 1) * eighth]
        other = packed[(k + NY) * eighth : (k + NY + 1) * eighth]
        proj = proj + dot(near[k], mine, 0, 0)
        proj = proj + dot(far[k], other, 0, 0)
    proj = proj.astype(BF)
    grad_proj = lax.psum_scatter(proj, Z, scatter_dimension=0, tiled=True)
    grad_out = after(jnp.concatenate(near + far, 0), proj)
    back = dot(grad_out, weights, 1, 0, BF)
    total = dot(unpick[0], back, 1, 0)
    for k in range(1, NX):
        part = dot(unpick[k], back, 1, 0, BF)
        total = total + shift(part, "x", NX, -k).astype(F32)
    return total.astype(BF), grad_proj.astype(F32)


def body(
    cache_keys,
    cache_values,
    step_queries,
    step_keys,
    step_values,
    reward_head,
    lengths,
    assign,
    response_feats,
    out_proj,
    loss_probe,
):
    local_rows, slots, width_local = response_feats.shape
    total_rows = lengths.shape[0]
    shards = lax.axis_size(S)
    my_shard = lax.axis_index(S)
    zhi, xx, zlo = lax.axis_index("zhi"), lax.axis_index("x"), lax.axis_index("zlo")
    full = local_rows * slots
    few = 304
    section_full = NX * full
    section_few = 1024
    weights = lax.all_gather(out_proj, Z, axis=0, tiled=True)

    steps = jnp.arange(slots)
    targets = lax.dynamic_slice_in_dim(assign, my_shard * local_rows, local_rows) // local_rows
    goes = (targets[:, None] * slots + steps[None, :]).reshape(1, -1)
    placing = (jnp.arange(shards * slots)[:, None] == goes).astype(BF)
    outgoing = dot(placing, response_feats.reshape(full, width_local), 1, 0, BF)
    step_queries, outgoing = lax.optimization_barrier((step_queries, outgoing))
    incoming = lax.all_to_all(outgoing, S, split_axis=0, concat_axis=0, tiled=True)

    decoded = decode_rows(step_queries, cache_keys, cache_values, step_keys, step_values)
    head_terms = jnp.dot(
        decoded.reshape(local_rows * STEPS, width_local),
        reward_head,
        preferred_element_type=F32,
    )
    head_terms = head_terms.reshape(local_rows, STEPS).sum(1) / STEPS

    ids = jnp.arange(NX * local_rows)
    shard = (zhi * NX + (xx - ids // local_rows) % NX) * 2 + zlo
    slot = shard * local_rows + ids % local_rows
    found = assign[None, :] == slot[:, None]
    all_rows = jnp.arange(total_rows)
    row_len = jnp.sum(jnp.where(found, lengths[None, :], 0), 1)
    from_shard = jnp.sum(jnp.where(found[:local_rows], (all_rows // local_rows)[None, :], 0), 1)
    own_len = row_len[:local_rows]
    own_ids = jnp.arange(local_rows)
    own_start = jnp.sum(
        jnp.where(own_ids[None, :] < own_ids[:, None], own_len[None, :], 0), 1
    )
    comes = from_shard[None, :] == jnp.arange(shards)[:, None]
    src_start = jnp.sum(jnp.where(comes, own_start[None, :], 0), 1)
    src_len = jnp.sum(jnp.where(comes, own_len[None, :], 0), 1)
    lies = jnp.where(
        steps[None, :] < src_len[:, None], src_start[:, None] + steps[None, :], -1
    ).reshape(1, -1)
    wants = jnp.where(
        steps[None, :] < own_len[:, None], own_start[:, None] + steps[None, :], -1
    ).reshape(-1, 1)
    picking = (jnp.arange(few)[:, None] == lies).astype(BF)
    leaving = (wants == jnp.arange(few)[None, :]).astype(BF)

    shard_len = jnp.sum(row_len.reshape(NX, local_rows), 1)
    capped = jnp.minimum(shard_len, few)
    blocks = jnp.arange(NX)
    ahead = jnp.sum(jnp.where(blocks[None, :] < blocks[:, None], capped[None, :], 0), 1)
    taken = jnp.clip(section_few - ahead, 0, capped)
    pick, unpick, rows_of = section_plan(
        section_few, few, slots, row_len, jnp.zeros_like(taken), taken
    )
    loads = jnp.sum(
        jnp.where(
            (assign // local_rows)[None, :] == jnp.arange(shards)[:, None], lengths[None, :], 0
        ),
        1,
    )
    sections = loads.reshape(4, NX, 2).sum(1)
    more = (jnp.max(loads) > few) | (jnp.max(sections) > section_few)
    row_rewards = sum_mp(head_terms)
    masks = (pick, unpick, picking, leaving, rows_of, row_len, more)
    masks, incoming, row_rewards = lax.optimization_barrier((masks, incoming, row_rewards))
    pick, unpick, picking, leaving, rows_of, row_len, more = masks
    own = dot(picking, incoming, 1, 0, BF)
    feats = gather_x(own)
    rewards = share_small(after(row_rewards, own), S).reshape(-1)
    feats[2], rewards, weights = lax.optimization_barrier((feats[2], rewards, weights))
    here, packed = forward(feats, weights, pick)

    groups = total_rows // GROUP
    group_mean = rewards.reshape(GROUP, groups).mean(0)
    advantages = rewards - jnp.tile(group_mean, GROUP)
    row_adv = jnp.sum(jnp.where(found, advantages[None, :], 0.0), 1)
    row_coef = row_adv / row_len.astype(F32)
    per_shard = loss_probe.shape[0] // shards
    probe = lax.dynamic_index_in_dim(
        loss_probe.reshape(4, NX, 2 * per_shard), xx, 1, keepdims=False
    ).reshape(-1)

    coef = jnp.sum(jnp.where(rows_of, row_coef[None, :], 0.0), 1)
    grad_mine = grad_output(sum_y(here), coef, probe)
    total, grad_proj = backward(grad_mine, packed, weights, unpick)
    grad_own = dot(leaving, total, 1, 0, BF)

    def rest(args):
        grad_own, grad_proj, incoming, weights, row_coef, probe, lies, wants = args
        rest_tokens = section_full - section_few
        pick, unpick, rows_of = section_plan(
            rest_tokens, full, slots, row_len, taken, shard_len
        )
        picking = (jnp.arange(full)[:, None] == lies).astype(BF)
        leaving = (wants == jnp.arange(full)[None, :]).astype(BF)
        feats = gather_x(dot(picking, incoming, 1, 0, BF))
        here, packed = forward(feats, weights, pick)
        coef = jnp.sum(jnp.where(rows_of, row_coef[None, :], 0.0), 1)
        grad_mine = grad_output(sum_y(here), coef, probe)
        total, proj = backward(grad_mine, packed, weights, unpick)
        return grad_own + dot(leaving, total, 1, 0, BF), grad_proj + proj

    grad_own, grad_proj = lax.cond(
        more,
        rest,
        lambda args: (args[0], args[1]),
        (grad_own, grad_proj, incoming, weights, row_coef, probe, lies, wants),
    )
    grad_features = grad_own.reshape(local_rows, slots, width_local)
    return (advantages, grad_features, grad_proj)


def solution(mesh):
    fine = Mesh(
        mesh.devices.reshape(4, NX, 2, NY, 2), ("zhi", "x", "zlo", "y", "core")
    )
    rows3 = P(S, None, MP)
    placed = (
        rows3,
        rows3,
        rows3,
        rows3,
        rows3,
        P(MP),
        P(),
        P(),
        rows3,
        P(S, MP),
        P(),
    )
    return jax.shard_map(
        body,
        mesh=fine,
        in_specs=placed,
        out_specs=(P(), rows3, P(S, MP)),
        check_vma=False,
    )
```

```python
import math

import jax
import jax.numpy as jnp
from jax import lax
from jax.sharding import Mesh
from jax.sharding import PartitionSpec as P

HD = 128
STEPS = 4
GROUP = 16
NX = 4
NY = 4
Z = ("zhi", "zlo")
S = ("zhi", "x", "zlo")
MP = ("y", "core")
BF = jnp.bfloat16
F32 = jnp.float32


def decode_rows(step_queries, cache_keys, cache_values, step_keys, step_values):
    rows = step_queries.shape[0]
    kv_local = cache_keys.shape[2] // HD
    heads_local = step_queries.shape[2] // HD
    share = heads_local // kv_local
    context = cache_keys.shape[1]
    queries = step_queries.reshape(rows, STEPS, kv_local, share, HD)
    keys_far = cache_keys.reshape(rows, context, kv_local, HD)
    values_far = cache_values.reshape(rows, context, kv_local, HD)
    keys_near = step_keys.reshape(rows, STEPS, kv_local, HD)
    values_near = step_values.reshape(rows, STEPS, kv_local, HD)
    scale = 1.0 / math.sqrt(HD)
    far = (
        jnp.einsum("rskgh,rckh->rksgc", queries, keys_far, preferred_element_type=F32)
        * scale
    )
    near = (
        jnp.einsum("rskgh,rjkh->rksgj", queries, keys_near, preferred_element_type=F32)
        * scale
    )
    causal = (jnp.arange(STEPS)[None, :] <= jnp.arange(STEPS)[:, None])[None, None, :, None, :]
    near = jnp.where(causal, near, -jnp.inf)
    top = jnp.maximum(far.max(-1), near.max(-1))[..., None]
    far_exp = jnp.exp(far - top)
    near_exp = jnp.exp(near - top)
    total = far_exp.sum(-1, keepdims=True) + near_exp.sum(-1, keepdims=True)
    far_w = (far_exp / total).astype(BF)
    near_w = (near_exp / total).astype(BF)
    mixed = jnp.einsum("rksgc,rckh->rskgh", far_w, values_far, preferred_element_type=F32)
    mixed = mixed + jnp.einsum(
        "rksgj,rjkh->rskgh", near_w, values_near, preferred_element_type=F32
    )
    return mixed.reshape(rows, STEPS, heads_local * HD).astype(BF)


def grad_output(outputs, probe_part):
    sig = jax.nn.sigmoid(outputs)
    return (probe_part.astype(F32)[None, :] * (sig * (1.0 + outputs * (1.0 - sig)))).astype(BF)


def shift(value, axis, size, by):
    return lax.ppermute(value, axis, [(i, (i + by) % size) for i in range(size)])


def swap(value):
    return lax.ppermute(value, "core", [(0, 1), (1, 0)])


def share_small(vector, axes):
    count = lax.axis_size(axes)
    tile = jnp.pad(vector[None, :], ((0, 7), (0, 128 - vector.shape[0])))
    copies = jnp.broadcast_to(tile[None], (count,) + tile.shape)
    got = lax.all_to_all(copies, axes, split_axis=0, concat_axis=0, tiled=True)
    return got[:, 0, : vector.shape[0]]


def after(value, earlier):
    return lax.optimization_barrier((value, earlier))[0]


def dot(a, b, ca, cb, out=F32):
    return lax.dot_general(
        a, b, (((ca,), (cb,)), ((), ())), preferred_element_type=F32
    ).astype(out)


def section_plan(tokens, per, slots, row_len, low, high):
    start = row_len.reshape(NX, -1)
    count = start.shape[1]
    ids = jnp.arange(count)
    before = ids[None, None, :] < ids[None, :, None]
    start = jnp.sum(jnp.where(before, start[:, None, :], 0), 2)
    blocks = jnp.arange(NX)
    base = jnp.sum(
        jnp.where(blocks[None, :] < blocks[:, None], (high - low)[None, :], 0), 1
    )
    spot = jnp.arange(per)[None, :]
    place = jnp.where(
        (spot >= low[:, None]) & (spot < high[:, None]), (base - low)[:, None] + spot, -1
    ).reshape(-1)
    ends = jnp.minimum(start + row_len.reshape(NX, -1), high[:, None])
    first = jnp.maximum(start, low[:, None])
    run_start = ((base - low)[:, None] + first).reshape(-1)
    run_end = run_start + jnp.maximum(ends - first, 0).reshape(-1)
    half = tokens // 2
    eighth = tokens // 8
    j = jnp.arange(tokens)
    owner_core = lax.axis_index("core") ^ (j // half)
    owner_y = (lax.axis_index("y") + (j % half) // eighth) % NY
    q = (owner_core * NY + owner_y) * eighth + j % eighth
    pick = (q[:, None] == place[None, :]).astype(BF)
    unpick = (place[:, None] == q[None, :]).astype(BF)
    rows_of = (run_start[None, :] <= q[:, None]) & (q[:, None] < run_end[None, :])
    return pick, unpick, rows_of


def gather_x(own):
    return jnp.concatenate([own] + [shift(own, "x", NX, k) for k in range(1, NX)], 0)


def forward(tokens, feats, weights, pick):
    half = tokens // 2
    packed_away = dot(pick[half:], feats, 1, 0, BF)
    away = swap(dot(packed_away, weights, 1, 1, BF))
    packed_here = dot(pick[:half], feats, 1, 0, BF)
    here = dot(packed_here, weights, 1, 1) + away.astype(F32)
    return here, packed_here, packed_away


def sum_y(here):
    eighth = here.shape[0] // NY
    outputs = here[:eighth]
    parts = []
    for k in range(1, NY):
        block = here[k * eighth : (k + 1) * eighth].astype(BF)
        parts.append(shift(block, "y", NY, k))
        outputs = outputs + parts[-1].astype(F32)
    return outputs, parts[0]


def token_scale(rows_of, row_coef):
    return jnp.sum(jnp.where(rows_of, row_coef[None, :], 0.0), 1)[:, None]


def backward(grad_mine, packed_here, packed_away, weights, unpick, scale, own_scale):
    parts = [grad_mine] + [shift(grad_mine, "y", NY, -k) for k in range(1, NY)]
    grad_here = jnp.concatenate(parts, 0)
    grad_away = jnp.concatenate([swap(part) for part in parts], 0)
    half = grad_here.shape[0]
    packed_here = (packed_here.astype(F32) * scale[:half]).astype(BF)
    packed_away = (packed_away.astype(F32) * scale[half:]).astype(BF)
    proj = dot(grad_here, packed_here, 0, 0) + dot(grad_away, packed_away, 0, 0)
    grad_proj = lax.psum_scatter(proj.astype(BF), Z, scatter_dimension=0, tiled=True)
    back = jnp.concatenate(
        [dot(grad_here, weights, 1, 0, BF), dot(grad_away, weights, 1, 0, BF)], 0
    )
    per = unpick.shape[0] // NX
    total = dot(unpick[:per], back, 1, 0)
    for k in range(1, NX):
        part = dot(unpick[k * per : (k + 1) * per], back, 1, 0, BF)
        total = total + shift(part, "x", NX, -k).astype(F32)
    return (total * own_scale).astype(BF), grad_proj.astype(F32)


def body(
    cache_keys,
    cache_values,
    step_queries,
    step_keys,
    step_values,
    reward_head,
    lengths,
    assign,
    response_feats,
    out_proj,
    loss_probe,
):
    local_rows, slots, width_local = response_feats.shape
    total_rows = lengths.shape[0]
    shards = lax.axis_size(S)
    my_shard = lax.axis_index(S)
    zhi, xx, zlo = lax.axis_index("zhi"), lax.axis_index("x"), lax.axis_index("zlo")
    full = local_rows * slots
    few = 304
    section_full = NX * full
    section_few = 1024
    weights = lax.all_gather(out_proj, Z, axis=0, tiled=True)

    steps = jnp.arange(slots)
    targets = lax.dynamic_slice_in_dim(assign, my_shard * local_rows, local_rows) // local_rows
    goes = (targets[:, None] * slots + steps[None, :]).reshape(1, -1)
    placing = (jnp.arange(shards * slots)[:, None] == goes).astype(BF)
    outgoing = dot(placing, response_feats.reshape(full, width_local), 1, 0, BF)
    step_queries, outgoing = lax.optimization_barrier((step_queries, outgoing))
    incoming = lax.all_to_all(outgoing, S, split_axis=0, concat_axis=0, tiled=True)

    decoded = decode_rows(step_queries, cache_keys, cache_values, step_keys, step_values)
    head_terms = jnp.dot(
        decoded.reshape(local_rows * STEPS, width_local),
        reward_head,
        preferred_element_type=F32,
    )
    head_terms = head_terms.reshape(local_rows, STEPS).sum(1) / STEPS

    ids = jnp.arange(NX * local_rows)
    shard = (zhi * NX + (xx - ids // local_rows) % NX) * 2 + zlo
    slot = shard * local_rows + ids % local_rows
    found = assign[None, :] == slot[:, None]
    all_rows = jnp.arange(total_rows)
    row_len = jnp.sum(jnp.where(found, lengths[None, :], 0), 1)
    from_shard = jnp.sum(jnp.where(found[:local_rows], (all_rows // local_rows)[None, :], 0), 1)
    own_len = row_len[:local_rows]
    own_ids = jnp.arange(local_rows)
    own_start = jnp.sum(
        jnp.where(own_ids[None, :] < own_ids[:, None], own_len[None, :], 0), 1
    )
    comes = from_shard[None, :] == jnp.arange(shards)[:, None]
    src_start = jnp.sum(jnp.where(comes, own_start[None, :], 0), 1)
    src_len = jnp.sum(jnp.where(comes, own_len[None, :], 0), 1)
    lies = jnp.where(
        steps[None, :] < src_len[:, None], src_start[:, None] + steps[None, :], -1
    ).reshape(1, -1)
    wants = jnp.where(
        steps[None, :] < own_len[:, None], own_start[:, None] + steps[None, :], -1
    ).reshape(-1, 1)
    picking = (jnp.arange(few)[:, None] == lies).astype(BF)
    leaving = (wants == jnp.arange(few)[None, :]).astype(BF)

    shard_len = jnp.sum(row_len.reshape(NX, local_rows), 1)
    capped = jnp.minimum(shard_len, few)
    blocks = jnp.arange(NX)
    ahead = jnp.sum(jnp.where(blocks[None, :] < blocks[:, None], capped[None, :], 0), 1)
    taken = jnp.clip(section_few - ahead, 0, capped)
    pick, unpick, rows_of = section_plan(
        section_few, few, slots, row_len, jnp.zeros_like(taken), taken
    )
    loads = jnp.sum(
        jnp.where(
            (assign // local_rows)[None, :] == jnp.arange(shards)[:, None], lengths[None, :], 0
        ),
        1,
    )
    sections = loads.reshape(4, NX, 2).sum(1)
    more = (jnp.max(loads) > few) | (jnp.max(sections) > section_few)
    pick, unpick, picking, leaving, incoming, head_terms, more = lax.optimization_barrier(
        (pick, unpick, picking, leaving, incoming, head_terms, more)
    )
    own = dot(picking, incoming, 1, 0, BF)
    own, head_terms = lax.optimization_barrier((own, head_terms))
    row_rewards = share_small(head_terms, MP).sum(0)
    feats, row_rewards, weights = lax.optimization_barrier(
        (gather_x(own), row_rewards, weights)
    )
    here, packed_here, packed_away = forward(section_few, feats, weights, pick)

    outputs, first = sum_y(here)
    rewards = share_small(after(row_rewards, first), S).reshape(-1)
    groups = total_rows // GROUP
    group_mean = rewards.reshape(GROUP, groups).mean(0)
    advantages = rewards - jnp.tile(group_mean, GROUP)
    row_adv = jnp.sum(jnp.where(found, advantages[None, :], 0.0), 1)
    row_coef = row_adv / row_len.astype(F32)
    per_shard = loss_probe.shape[0] // shards
    probe = lax.dynamic_index_in_dim(
        loss_probe.reshape(4, NX, 2 * per_shard), xx, 1, keepdims=False
    ).reshape(-1)

    def own_scale(count):
        spot = jnp.arange(count)[:, None]
        own_rows = (own_start[None, :] <= spot) & (spot < (own_start + own_len)[None, :])
        return token_scale(own_rows, row_coef[:local_rows])

    total, grad_proj = backward(
        grad_output(outputs, probe),
        packed_here,
        packed_away,
        weights,
        unpick,
        token_scale(rows_of, row_coef),
        own_scale(few),
    )
    grad_own = dot(leaving, total, 1, 0, BF)

    def rest(args):
        grad_own, grad_proj, incoming, weights, row_coef, probe, lies, wants = args
        rest_tokens = section_full - section_few
        pick, unpick, rows_of = section_plan(
            rest_tokens, full, slots, row_len, taken, shard_len
        )
        picking = (jnp.arange(full)[:, None] == lies).astype(BF)
        leaving = (wants == jnp.arange(full)[None, :]).astype(BF)
        feats = gather_x(dot(picking, incoming, 1, 0, BF))
        here, packed_here, packed_away = forward(rest_tokens, feats, weights, pick)
        outputs, _ = sum_y(here)
        total, proj = backward(
            grad_output(outputs, probe),
            packed_here,
            packed_away,
            weights,
            unpick,
            token_scale(rows_of, row_coef),
            own_scale(full),
        )
        return grad_own + dot(leaving, total, 1, 0, BF), grad_proj + proj

    grad_own, grad_proj = lax.cond(
        more,
        rest,
        lambda args: (args[0], args[1]),
        (grad_own, grad_proj, incoming, weights, row_coef, probe, lies, wants),
    )
    grad_features = grad_own.reshape(local_rows, slots, width_local)
    return (advantages, grad_features, grad_proj)


def solution(mesh):
    fine = Mesh(
        mesh.devices.reshape(4, NX, 2, NY, 2), ("zhi", "x", "zlo", "y", "core")
    )
    rows3 = P(S, None, MP)
    placed = (
        rows3,
        rows3,
        rows3,
        rows3,
        rows3,
        P(MP),
        P(),
        P(),
        rows3,
        P(S, MP),
        P(),
    )
    return jax.shard_map(
        body,
        mesh=fine,
        in_specs=placed,
        out_specs=(P(), rows3, P(S, MP)),
        check_vma=False,
    )
```

```python
import math

import jax
import jax.numpy as jnp
from jax import lax
from jax.sharding import Mesh
from jax.sharding import PartitionSpec as P

HD = 128
STEPS = 4
GROUP = 16
NX = 4
NY = 4
Z = ("zhi", "zlo")
S = ("zhi", "x", "zlo")
MP = ("y", "core")
BF = jnp.bfloat16
F32 = jnp.float32


def decode_rows(step_queries, cache_keys, cache_values, step_keys, step_values):
    rows = step_queries.shape[0]
    kv_local = cache_keys.shape[2] // HD
    heads_local = step_queries.shape[2] // HD
    share = heads_local // kv_local
    context = cache_keys.shape[1]
    queries = step_queries.reshape(rows, STEPS, kv_local, share, HD)
    keys_far = cache_keys.reshape(rows, context, kv_local, HD)
    values_far = cache_values.reshape(rows, context, kv_local, HD)
    keys_near = step_keys.reshape(rows, STEPS, kv_local, HD)
    values_near = step_values.reshape(rows, STEPS, kv_local, HD)
    scale = 1.0 / math.sqrt(HD)
    far = (
        jnp.einsum("rskgh,rckh->rksgc", queries, keys_far, preferred_element_type=F32)
        * scale
    )
    near = (
        jnp.einsum("rskgh,rjkh->rksgj", queries, keys_near, preferred_element_type=F32)
        * scale
    )
    causal = (jnp.arange(STEPS)[None, :] <= jnp.arange(STEPS)[:, None])[None, None, :, None, :]
    near = jnp.where(causal, near, -jnp.inf)
    top = jnp.maximum(far.max(-1), near.max(-1))[..., None]
    far_exp = jnp.exp(far - top)
    near_exp = jnp.exp(near - top)
    total = far_exp.sum(-1, keepdims=True) + near_exp.sum(-1, keepdims=True)
    far_w = (far_exp / total).astype(BF)
    near_w = (near_exp / total).astype(BF)
    mixed = jnp.einsum("rksgc,rckh->rskgh", far_w, values_far, preferred_element_type=F32)
    mixed = mixed + jnp.einsum(
        "rksgj,rjkh->rskgh", near_w, values_near, preferred_element_type=F32
    )
    return mixed.reshape(rows, STEPS, heads_local * HD).astype(BF)


def grad_output(outputs, probe_part):
    sig = jax.nn.sigmoid(outputs)
    return (probe_part.astype(F32)[None, :] * (sig * (1.0 + outputs * (1.0 - sig)))).astype(BF)


def shift(value, axis, size, by):
    return lax.ppermute(value, axis, [(i, (i + by) % size) for i in range(size)])


def swap(value):
    return lax.ppermute(value, "core", [(0, 1), (1, 0)])


def share_small(vector, axes):
    count = lax.axis_size(axes)
    tile = jnp.pad(vector[None, :], ((0, 7), (0, 128 - vector.shape[0])))
    copies = jnp.broadcast_to(tile[None], (count,) + tile.shape)
    got = lax.all_to_all(copies, axes, split_axis=0, concat_axis=0, tiled=True)
    return got[:, 0, : vector.shape[0]]


def after(value, earlier):
    return lax.optimization_barrier((value, earlier))[0]


def dot(a, b, ca, cb, out=F32):
    return lax.dot_general(
        a, b, (((ca,), (cb,)), ((), ())), preferred_element_type=F32
    ).astype(out)


def section_plan(tokens, per, slots, row_len, low, high):
    start = row_len.reshape(NX, -1)
    count = start.shape[1]
    ids = jnp.arange(count)
    before = ids[None, None, :] < ids[None, :, None]
    start = jnp.sum(jnp.where(before, start[:, None, :], 0), 2)
    blocks = jnp.arange(NX)
    base = jnp.sum(
        jnp.where(blocks[None, :] < blocks[:, None], (high - low)[None, :], 0), 1
    )
    spot = jnp.arange(per)[None, :]
    place = jnp.where(
        (spot >= low[:, None]) & (spot < high[:, None]), (base - low)[:, None] + spot, -1
    ).reshape(-1)
    ends = jnp.minimum(start + row_len.reshape(NX, -1), high[:, None])
    first = jnp.maximum(start, low[:, None])
    run_start = ((base - low)[:, None] + first).reshape(-1)
    run_end = run_start + jnp.maximum(ends - first, 0).reshape(-1)
    half = tokens // 2
    eighth = tokens // 8
    j = jnp.arange(tokens)
    owner_core = lax.axis_index("core") ^ (j // half)
    owner_y = (lax.axis_index("y") + (j % half) // eighth) % NY
    q = (owner_core * NY + owner_y) * eighth + j % eighth
    pick = (q[:, None] == place[None, :]).astype(BF)
    unpick = (place[:, None] == q[None, :]).astype(BF)
    rows_of = (run_start[None, :] <= q[:, None]) & (q[:, None] < run_end[None, :])
    return pick, unpick, rows_of


def gather_x(own):
    return jnp.concatenate([own] + [shift(own, "x", NX, k) for k in range(1, NX)], 0)


def forward(tokens, feats, weights, pick, packed_away):
    half = tokens // 2
    away = swap(dot(packed_away, weights, 1, 1, BF))
    packed_here = dot(pick[:half], feats, 1, 0, BF)
    here = dot(packed_here, weights, 1, 1) + away.astype(F32)
    return here, packed_here, packed_away


def sum_y(here):
    eighth = here.shape[0] // NY
    outputs = here[:eighth]
    parts = []
    for k in range(1, NY):
        block = here[k * eighth : (k + 1) * eighth].astype(BF)
        parts.append(shift(block, "y", NY, k))
        outputs = outputs + parts[-1].astype(F32)
    return outputs, parts[0]


def token_scale(rows_of, row_coef):
    return jnp.sum(jnp.where(rows_of, row_coef[None, :], 0.0), 1)[:, None]


def backward(grad_mine, packed_here, packed_away, weights, unpick, scale, own_scale):
    parts = [grad_mine] + [shift(grad_mine, "y", NY, -k) for k in range(1, NY)]
    grad_here = jnp.concatenate(parts, 0)
    grad_away = jnp.concatenate([swap(part) for part in parts], 0)
    half = grad_here.shape[0]
    packed_here = (packed_here.astype(F32) * scale[:half]).astype(BF)
    packed_away = (packed_away.astype(F32) * scale[half:]).astype(BF)
    proj = dot(grad_here, packed_here, 0, 0) + dot(grad_away, packed_away, 0, 0)
    grad_proj = lax.psum_scatter(proj.astype(BF), Z, scatter_dimension=0, tiled=True)
    back = jnp.concatenate(
        [dot(grad_here, weights, 1, 0, BF), dot(grad_away, weights, 1, 0, BF)], 0
    )
    per = unpick.shape[0] // NX
    total = dot(unpick[:per], back, 1, 0)
    for k in range(1, NX):
        part = dot(unpick[k * per : (k + 1) * per], back, 1, 0, BF)
        total = total + shift(part, "x", NX, -k).astype(F32)
    return (total * own_scale).astype(BF), grad_proj.astype(F32)


def body(
    cache_keys,
    cache_values,
    step_queries,
    step_keys,
    step_values,
    reward_head,
    lengths,
    assign,
    response_feats,
    out_proj,
    loss_probe,
):
    local_rows, slots, width_local = response_feats.shape
    total_rows = lengths.shape[0]
    shards = lax.axis_size(S)
    my_shard = lax.axis_index(S)
    zhi, xx, zlo = lax.axis_index("zhi"), lax.axis_index("x"), lax.axis_index("zlo")
    full = local_rows * slots
    few = 304
    section_full = NX * full
    section_few = 1024

    steps = jnp.arange(slots)
    targets = lax.dynamic_slice_in_dim(assign, my_shard * local_rows, local_rows) // local_rows
    goes = (targets[:, None] * slots + steps[None, :]).reshape(1, -1)
    placing = (jnp.arange(shards * slots)[:, None] == goes).astype(BF)
    outgoing = dot(placing, response_feats.reshape(full, width_local), 1, 0, BF)
    step_queries, outgoing = lax.optimization_barrier((step_queries, outgoing))
    incoming = lax.all_to_all(outgoing, S, split_axis=0, concat_axis=0, tiled=True)

    decoded = decode_rows(step_queries, cache_keys, cache_values, step_keys, step_values)
    head_terms = jnp.dot(
        decoded.reshape(local_rows * STEPS, width_local),
        reward_head,
        preferred_element_type=F32,
    )
    head_terms = head_terms.reshape(local_rows, STEPS).sum(1) / STEPS

    weights = lax.all_gather(after(out_proj, head_terms), Z, axis=0, tiled=True)

    ids = jnp.arange(NX * local_rows)
    shard = (zhi * NX + (xx - ids // local_rows) % NX) * 2 + zlo
    slot = shard * local_rows + ids % local_rows
    found = assign[None, :] == slot[:, None]
    all_rows = jnp.arange(total_rows)
    row_len = jnp.sum(jnp.where(found, lengths[None, :], 0), 1)
    from_shard = jnp.sum(jnp.where(found[:local_rows], (all_rows // local_rows)[None, :], 0), 1)
    own_len = row_len[:local_rows]
    own_ids = jnp.arange(local_rows)
    own_start = jnp.sum(
        jnp.where(own_ids[None, :] < own_ids[:, None], own_len[None, :], 0), 1
    )
    comes = from_shard[None, :] == jnp.arange(shards)[:, None]
    src_start = jnp.sum(jnp.where(comes, own_start[None, :], 0), 1)
    src_len = jnp.sum(jnp.where(comes, own_len[None, :], 0), 1)
    lies = jnp.where(
        steps[None, :] < src_len[:, None], src_start[:, None] + steps[None, :], -1
    ).reshape(1, -1)
    wants = jnp.where(
        steps[None, :] < own_len[:, None], own_start[:, None] + steps[None, :], -1
    ).reshape(-1, 1)
    picking = (jnp.arange(few)[:, None] == lies).astype(BF)
    leaving = (wants == jnp.arange(few)[None, :]).astype(BF)

    shard_len = jnp.sum(row_len.reshape(NX, local_rows), 1)
    capped = jnp.minimum(shard_len, few)
    blocks = jnp.arange(NX)
    ahead = jnp.sum(jnp.where(blocks[None, :] < blocks[:, None], capped[None, :], 0), 1)
    taken = jnp.clip(section_few - ahead, 0, capped)
    pick, unpick, rows_of = section_plan(
        section_few, few, slots, row_len, jnp.zeros_like(taken), taken
    )
    loads = jnp.sum(
        jnp.where(
            (assign // local_rows)[None, :] == jnp.arange(shards)[:, None], lengths[None, :], 0
        ),
        1,
    )
    sections = loads.reshape(4, NX, 2).sum(1)
    more = (jnp.max(loads) > few) | (jnp.max(sections) > section_few)
    row_rewards = lax.psum(head_terms, MP)
    pick, unpick, picking, leaving, incoming, row_rewards = lax.optimization_barrier(
        (pick, unpick, picking, leaving, incoming, row_rewards)
    )
    own = dot(picking, incoming, 1, 0, BF)
    rewards = share_small(after(row_rewards, own), S).reshape(-1)
    feats, weights = lax.optimization_barrier((gather_x(own), weights))
    packed_away = dot(pick[section_few // 2 :], feats, 1, 0, BF)
    packed_away, rewards = lax.optimization_barrier((packed_away, rewards))
    here, packed_here, packed_away = forward(
        section_few, feats, weights, pick, packed_away
    )

    outputs, first = sum_y(here)
    groups = total_rows // GROUP
    group_mean = rewards.reshape(GROUP, groups).mean(0)
    advantages = rewards - jnp.tile(group_mean, GROUP)
    row_adv = jnp.sum(jnp.where(found, advantages[None, :], 0.0), 1)
    row_coef = row_adv / row_len.astype(F32)
    per_shard = loss_probe.shape[0] // shards
    probe = lax.dynamic_index_in_dim(
        loss_probe.reshape(4, NX, 2 * per_shard), xx, 1, keepdims=False
    ).reshape(-1)

    def own_scale(count):
        spot = jnp.arange(count)[:, None]
        own_rows = (own_start[None, :] <= spot) & (spot < (own_start + own_len)[None, :])
        return token_scale(own_rows, row_coef[:local_rows])

    total, grad_proj = backward(
        grad_output(outputs, probe),
        packed_here,
        packed_away,
        weights,
        unpick,
        token_scale(rows_of, row_coef),
        own_scale(few),
    )
    grad_own = dot(leaving, total, 1, 0, BF)

    def rest(args):
        grad_own, grad_proj, incoming, weights, row_coef, probe, lies, wants = args
        rest_tokens = section_full - section_few
        pick, unpick, rows_of = section_plan(
            rest_tokens, full, slots, row_len, taken, shard_len
        )
        picking = (jnp.arange(full)[:, None] == lies).astype(BF)
        leaving = (wants == jnp.arange(full)[None, :]).astype(BF)
        feats = gather_x(dot(picking, incoming, 1, 0, BF))
        packed_away = dot(pick[rest_tokens // 2 :], feats, 1, 0, BF)
        here, packed_here, packed_away = forward(
            rest_tokens, feats, weights, pick, packed_away
        )
        outputs, _ = sum_y(here)
        total, proj = backward(
            grad_output(outputs, probe),
            packed_here,
            packed_away,
            weights,
            unpick,
            token_scale(rows_of, row_coef),
            own_scale(full),
        )
        return grad_own + dot(leaving, total, 1, 0, BF), grad_proj + proj

    grad_own, grad_proj = lax.cond(
        more,
        rest,
        lambda args: (args[0], args[1]),
        (grad_own, grad_proj, incoming, weights, row_coef, probe, lies, wants),
    )
    grad_features = grad_own.reshape(local_rows, slots, width_local)
    return (advantages, grad_features, grad_proj)


def solution(mesh):
    fine = Mesh(
        mesh.devices.reshape(4, NX, 2, NY, 2), ("zhi", "x", "zlo", "y", "core")
    )
    rows3 = P(S, None, MP)
    placed = (
        rows3,
        rows3,
        rows3,
        rows3,
        rows3,
        P(MP),
        P(),
        P(),
        rows3,
        P(S, MP),
        P(),
    )
    return jax.shard_map(
        body,
        mesh=fine,
        in_specs=placed,
        out_specs=(P(), rows3, P(S, MP)),
        check_vma=False,
    )
```

```python
import math

import jax
import jax.numpy as jnp
from jax import lax
from jax.sharding import Mesh
from jax.sharding import PartitionSpec as P

HD = 128
STEPS = 4
GROUP = 16
NX = 4
NY = 4
Z = ("zhi", "zlo")
S = ("zhi", "x", "zlo")
MP = ("y", "core")
BF = jnp.bfloat16
F32 = jnp.float32


def decode_rows(step_queries, cache_keys, cache_values, step_keys, step_values):
    rows = step_queries.shape[0]
    kv_local = cache_keys.shape[2] // HD
    heads_local = step_queries.shape[2] // HD
    share = heads_local // kv_local
    context = cache_keys.shape[1]
    queries = step_queries.reshape(rows, STEPS, kv_local, share, HD)
    keys_far = cache_keys.reshape(rows, context, kv_local, HD)
    values_far = cache_values.reshape(rows, context, kv_local, HD)
    keys_near = step_keys.reshape(rows, STEPS, kv_local, HD)
    values_near = step_values.reshape(rows, STEPS, kv_local, HD)
    scale = 1.0 / math.sqrt(HD)
    far = (
        jnp.einsum("rskgh,rckh->rksgc", queries, keys_far, preferred_element_type=F32)
        * scale
    )
    near = (
        jnp.einsum("rskgh,rjkh->rksgj", queries, keys_near, preferred_element_type=F32)
        * scale
    )
    causal = (jnp.arange(STEPS)[None, :] <= jnp.arange(STEPS)[:, None])[None, None, :, None, :]
    near = jnp.where(causal, near, -jnp.inf)
    top = jnp.maximum(far.max(-1), near.max(-1))[..., None]
    far_exp = jnp.exp(far - top)
    near_exp = jnp.exp(near - top)
    total = far_exp.sum(-1, keepdims=True) + near_exp.sum(-1, keepdims=True)
    far_w = (far_exp / total).astype(BF)
    near_w = (near_exp / total).astype(BF)
    mixed = jnp.einsum("rksgc,rckh->rskgh", far_w, values_far, preferred_element_type=F32)
    mixed = mixed + jnp.einsum(
        "rksgj,rjkh->rskgh", near_w, values_near, preferred_element_type=F32
    )
    return mixed.reshape(rows, STEPS, heads_local * HD).astype(BF)


def grad_output(outputs, probe_part):
    sig = jax.nn.sigmoid(outputs)
    return (probe_part.astype(F32)[None, :] * (sig * (1.0 + outputs * (1.0 - sig)))).astype(BF)


def shift(value, axis, size, by):
    return lax.ppermute(value, axis, [(i, (i + by) % size) for i in range(size)])


def swap(value):
    return lax.ppermute(value, "core", [(0, 1), (1, 0)])


def share_small(vector, axes):
    count = lax.axis_size(axes)
    tile = jnp.pad(vector[None, :], ((0, 7), (0, 128 - vector.shape[0])))
    copies = jnp.broadcast_to(tile[None], (count,) + tile.shape)
    got = lax.all_to_all(copies, axes, split_axis=0, concat_axis=0, tiled=True)
    return got[:, 0, : vector.shape[0]]


def after(value, earlier):
    return lax.optimization_barrier((value, earlier))[0]


def dot(a, b, ca, cb, out=F32):
    return lax.dot_general(
        a, b, (((ca,), (cb,)), ((), ())), preferred_element_type=F32
    ).astype(out)


def section_plan(tokens, per, slots, row_len, low, high):
    start = row_len.reshape(NX, -1)
    count = start.shape[1]
    ids = jnp.arange(count)
    before = ids[None, None, :] < ids[None, :, None]
    start = jnp.sum(jnp.where(before, start[:, None, :], 0), 2)
    blocks = jnp.arange(NX)
    base = jnp.sum(
        jnp.where(blocks[None, :] < blocks[:, None], (high - low)[None, :], 0), 1
    )
    spot = jnp.arange(per)[None, :]
    place = jnp.where(
        (spot >= low[:, None]) & (spot < high[:, None]), (base - low)[:, None] + spot, -1
    ).reshape(-1)
    ends = jnp.minimum(start + row_len.reshape(NX, -1), high[:, None])
    first = jnp.maximum(start, low[:, None])
    run_start = ((base - low)[:, None] + first).reshape(-1)
    run_end = run_start + jnp.maximum(ends - first, 0).reshape(-1)
    half = tokens // 2
    eighth = tokens // 8
    j = jnp.arange(tokens)
    owner_core = lax.axis_index("core") ^ (j // half)
    owner_y = (lax.axis_index("y") + (j % half) // eighth) % NY
    q = (owner_core * NY + owner_y) * eighth + j % eighth
    pick = (q[:, None] == place[None, :]).astype(BF)
    unpick = (place[:, None] == q[None, :]).astype(BF)
    rows_of = (run_start[None, :] <= q[:, None]) & (q[:, None] < run_end[None, :])
    return pick, unpick, rows_of


def gather_x(own):
    return jnp.concatenate([own] + [shift(own, "x", NX, k) for k in range(1, NX)], 0)


def forward(tokens, feats, weights, pick, packed_away):
    half = tokens // 2
    away = swap(dot(packed_away, weights, 1, 1, BF))
    packed_here = dot(pick[:half], feats, 1, 0, BF)
    here = dot(packed_here, weights, 1, 1) + away.astype(F32)
    return here, packed_here, packed_away


def sum_y(here):
    eighth = here.shape[0] // NY
    outputs = here[:eighth]
    parts = []
    for k in range(1, NY):
        block = here[k * eighth : (k + 1) * eighth].astype(BF)
        parts.append(shift(block, "y", NY, k))
        outputs = outputs + parts[-1].astype(F32)
    return outputs, parts[0]


def token_scale(rows_of, row_coef):
    return jnp.sum(jnp.where(rows_of, row_coef[None, :], 0.0), 1)[:, None]


def backward(grad_mine, packed_here, packed_away, weights, unpick, scale, own_scale):
    parts = [grad_mine] + [shift(grad_mine, "y", NY, -k) for k in range(1, NY)]
    grad_here = jnp.concatenate(parts, 0)
    grad_away = jnp.concatenate([swap(part) for part in parts], 0)
    half = grad_here.shape[0]
    packed_here = (packed_here.astype(F32) * scale[:half]).astype(BF)
    packed_away = (packed_away.astype(F32) * scale[half:]).astype(BF)
    proj = dot(grad_here, packed_here, 0, 0) + dot(grad_away, packed_away, 0, 0)
    grad_proj = lax.psum_scatter(proj.astype(BF), Z, scatter_dimension=0, tiled=True)
    back = jnp.concatenate(
        [dot(grad_here, weights, 1, 0, BF), dot(grad_away, weights, 1, 0, BF)], 0
    )
    per = unpick.shape[0] // NX
    total = dot(unpick[:per], back, 1, 0)
    for k in range(1, NX):
        part = dot(unpick[k * per : (k + 1) * per], back, 1, 0, BF)
        total = total + shift(part, "x", NX, -k).astype(F32)
    return (total * own_scale).astype(BF), grad_proj.astype(F32)


def body(
    cache_keys,
    cache_values,
    step_queries,
    step_keys,
    step_values,
    reward_head,
    lengths,
    assign,
    response_feats,
    out_proj,
    loss_probe,
):
    local_rows, slots, width_local = response_feats.shape
    total_rows = lengths.shape[0]
    shards = lax.axis_size(S)
    my_shard = lax.axis_index(S)
    zhi, xx, zlo = lax.axis_index("zhi"), lax.axis_index("x"), lax.axis_index("zlo")
    full = local_rows * slots
    few = 304
    section_full = NX * full
    section_few = 1024

    steps = jnp.arange(slots)
    targets = lax.dynamic_slice_in_dim(assign, my_shard * local_rows, local_rows) // local_rows
    goes = (targets[:, None] * slots + steps[None, :]).reshape(1, -1)
    placing = (jnp.arange(shards * slots)[:, None] == goes).astype(BF)
    outgoing = dot(placing, response_feats.reshape(full, width_local), 1, 0, BF)
    step_queries, outgoing = lax.optimization_barrier((step_queries, outgoing))
    incoming = lax.all_to_all(outgoing, S, split_axis=0, concat_axis=0, tiled=True)

    decoded = decode_rows(step_queries, cache_keys, cache_values, step_keys, step_values)
    head_terms = jnp.dot(
        decoded.reshape(local_rows * STEPS, width_local),
        reward_head,
        preferred_element_type=F32,
    )
    head_terms = head_terms.reshape(local_rows, STEPS).sum(1) / STEPS

    weights = lax.all_gather(after(out_proj, head_terms), Z, axis=0, tiled=True)

    ids = jnp.arange(NX * local_rows)
    shard = (zhi * NX + (xx - ids // local_rows) % NX) * 2 + zlo
    slot = shard * local_rows + ids % local_rows
    found = assign[None, :] == slot[:, None]
    all_rows = jnp.arange(total_rows)
    row_len = jnp.sum(jnp.where(found, lengths[None, :], 0), 1)
    from_shard = jnp.sum(jnp.where(found[:local_rows], (all_rows // local_rows)[None, :], 0), 1)
    own_len = row_len[:local_rows]
    own_ids = jnp.arange(local_rows)
    own_start = jnp.sum(
        jnp.where(own_ids[None, :] < own_ids[:, None], own_len[None, :], 0), 1
    )
    comes = from_shard[None, :] == jnp.arange(shards)[:, None]
    src_start = jnp.sum(jnp.where(comes, own_start[None, :], 0), 1)
    src_len = jnp.sum(jnp.where(comes, own_len[None, :], 0), 1)
    lies = jnp.where(
        steps[None, :] < src_len[:, None], src_start[:, None] + steps[None, :], -1
    ).reshape(1, -1)
    wants = jnp.where(
        steps[None, :] < own_len[:, None], own_start[:, None] + steps[None, :], -1
    ).reshape(-1, 1)
    picking = (jnp.arange(few)[:, None] == lies).astype(BF)
    leaving = (wants == jnp.arange(few)[None, :]).astype(BF)

    shard_len = jnp.sum(row_len.reshape(NX, local_rows), 1)
    capped = jnp.minimum(shard_len, few)
    blocks = jnp.arange(NX)
    ahead = jnp.sum(jnp.where(blocks[None, :] < blocks[:, None], capped[None, :], 0), 1)
    taken = jnp.clip(section_few - ahead, 0, capped)
    pick, unpick, rows_of = section_plan(
        section_few, few, slots, row_len, jnp.zeros_like(taken), taken
    )
    loads = jnp.sum(
        jnp.where(
            (assign // local_rows)[None, :] == jnp.arange(shards)[:, None], lengths[None, :], 0
        ),
        1,
    )
    sections = loads.reshape(4, NX, 2).sum(1)
    more = (jnp.max(loads) > few) | (jnp.max(sections) > section_few)
    row_rewards = lax.psum(head_terms, MP)
    pick, picking, incoming, row_rewards = lax.optimization_barrier(
        (pick, picking, incoming, row_rewards)
    )
    own = dot(picking, incoming, 1, 0, BF)
    rewards = share_small(after(row_rewards, own), S).reshape(-1)
    feats, weights = lax.optimization_barrier((gather_x(own), weights))
    packed_away = dot(pick[section_few // 2 :], feats, 1, 0, BF)
    packed_away, rewards = lax.optimization_barrier((packed_away, rewards))
    here, packed_here, packed_away = forward(
        section_few, feats, weights, pick, packed_away
    )

    outputs, first = sum_y(here)
    groups = total_rows // GROUP
    group_mean = rewards.reshape(GROUP, groups).mean(0)
    advantages = rewards - jnp.tile(group_mean, GROUP)
    row_adv = jnp.sum(jnp.where(found, advantages[None, :], 0.0), 1)
    row_coef = row_adv / row_len.astype(F32)
    per_shard = loss_probe.shape[0] // shards
    probe = lax.dynamic_index_in_dim(
        loss_probe.reshape(4, NX, 2 * per_shard), xx, 1, keepdims=False
    ).reshape(-1)

    def own_scale(count):
        spot = jnp.arange(count)[:, None]
        own_rows = (own_start[None, :] <= spot) & (spot < (own_start + own_len)[None, :])
        return token_scale(own_rows, row_coef[:local_rows])

    total, grad_proj = backward(
        grad_output(outputs, probe),
        packed_here,
        packed_away,
        weights,
        unpick,
        token_scale(rows_of, row_coef),
        own_scale(few),
    )
    grad_own = dot(leaving, total, 1, 0, BF)

    def rest(args):
        grad_own, grad_proj, incoming, weights, row_coef, probe, lies, wants = args
        rest_tokens = section_full - section_few
        pick, unpick, rows_of = section_plan(
            rest_tokens, full, slots, row_len, taken, shard_len
        )
        picking = (jnp.arange(full)[:, None] == lies).astype(BF)
        leaving = (wants == jnp.arange(full)[None, :]).astype(BF)
        feats = gather_x(dot(picking, incoming, 1, 0, BF))
        packed_away = dot(pick[rest_tokens // 2 :], feats, 1, 0, BF)
        here, packed_here, packed_away = forward(
            rest_tokens, feats, weights, pick, packed_away
        )
        outputs, _ = sum_y(here)
        total, proj = backward(
            grad_output(outputs, probe),
            packed_here,
            packed_away,
            weights,
            unpick,
            token_scale(rows_of, row_coef),
            own_scale(full),
        )
        return grad_own + dot(leaving, total, 1, 0, BF), grad_proj + proj

    grad_own, grad_proj = lax.cond(
        more,
        rest,
        lambda args: (args[0], args[1]),
        (grad_own, grad_proj, incoming, weights, row_coef, probe, lies, wants),
    )
    grad_features = grad_own.reshape(local_rows, slots, width_local)
    return (advantages, grad_features, grad_proj)


def solution(mesh):
    fine = Mesh(
        mesh.devices.reshape(4, NX, 2, NY, 2), ("zhi", "x", "zlo", "y", "core")
    )
    rows3 = P(S, None, MP)
    placed = (
        rows3,
        rows3,
        rows3,
        rows3,
        rows3,
        P(MP),
        P(),
        P(),
        rows3,
        P(S, MP),
        P(),
    )
    return jax.shard_map(
        body,
        mesh=fine,
        in_specs=placed,
        out_specs=(P(), rows3, P(S, MP)),
        check_vma=False,
    )
```

```python
import math

import jax
import jax.numpy as jnp
from jax import lax
from jax.sharding import Mesh
from jax.sharding import PartitionSpec as P

HD = 128
STEPS = 4
GROUP = 16
NX = 4
NY = 4
Z = ("zhi", "zlo")
S = ("zhi", "x", "zlo")
MP = ("y", "core")
BF = jnp.bfloat16
F32 = jnp.float32


def decode_rows(step_queries, cache_keys, cache_values, step_keys, step_values):
    rows = step_queries.shape[0]
    kv_local = cache_keys.shape[2] // HD
    heads_local = step_queries.shape[2] // HD
    share = heads_local // kv_local
    context = cache_keys.shape[1]
    queries = step_queries.reshape(rows, STEPS, kv_local, share, HD)
    keys_far = cache_keys.reshape(rows, context, kv_local, HD)
    values_far = cache_values.reshape(rows, context, kv_local, HD)
    keys_near = step_keys.reshape(rows, STEPS, kv_local, HD)
    values_near = step_values.reshape(rows, STEPS, kv_local, HD)
    scale = 1.0 / math.sqrt(HD)
    far = (
        jnp.einsum("rskgh,rckh->rksgc", queries, keys_far, preferred_element_type=F32)
        * scale
    )
    near = (
        jnp.einsum("rskgh,rjkh->rksgj", queries, keys_near, preferred_element_type=F32)
        * scale
    )
    causal = (jnp.arange(STEPS)[None, :] <= jnp.arange(STEPS)[:, None])[None, None, :, None, :]
    near = jnp.where(causal, near, -jnp.inf)
    top = jnp.maximum(far.max(-1), near.max(-1))[..., None]
    far_exp = jnp.exp(far - top)
    near_exp = jnp.exp(near - top)
    total = far_exp.sum(-1, keepdims=True) + near_exp.sum(-1, keepdims=True)
    far_w = (far_exp / total).astype(BF)
    near_w = (near_exp / total).astype(BF)
    mixed = jnp.einsum("rksgc,rckh->rskgh", far_w, values_far, preferred_element_type=F32)
    mixed = mixed + jnp.einsum(
        "rksgj,rjkh->rskgh", near_w, values_near, preferred_element_type=F32
    )
    return mixed.reshape(rows, STEPS, heads_local * HD).astype(BF)


def grad_output(outputs, probe_part):
    sig = jax.nn.sigmoid(outputs)
    return (probe_part.astype(F32)[None, :] * (sig * (1.0 + outputs * (1.0 - sig)))).astype(BF)


def shift(value, axis, size, by):
    return lax.ppermute(value, axis, [(i, (i + by) % size) for i in range(size)])


def swap(value):
    return lax.ppermute(value, "core", [(0, 1), (1, 0)])


def share_small(vector, axes):
    count = lax.axis_size(axes)
    tile = jnp.pad(vector[None, :], ((0, 7), (0, 128 - vector.shape[0])))
    copies = jnp.broadcast_to(tile[None], (count,) + tile.shape)
    got = lax.all_to_all(copies, axes, split_axis=0, concat_axis=0, tiled=True)
    return got[:, 0, : vector.shape[0]]


def after(value, earlier):
    return lax.optimization_barrier((value, earlier))[0]


def dot(a, b, ca, cb, out=F32):
    return lax.dot_general(
        a, b, (((ca,), (cb,)), ((), ())), preferred_element_type=F32
    ).astype(out)


def section_plan(tokens, per, slots, row_len, low, high):
    start = row_len.reshape(NX, -1)
    count = start.shape[1]
    ids = jnp.arange(count)
    before = ids[None, None, :] < ids[None, :, None]
    start = jnp.sum(jnp.where(before, start[:, None, :], 0), 2)
    blocks = jnp.arange(NX)
    base = jnp.sum(
        jnp.where(blocks[None, :] < blocks[:, None], (high - low)[None, :], 0), 1
    )
    spot = jnp.arange(per)[None, :]
    place = jnp.where(
        (spot >= low[:, None]) & (spot < high[:, None]), (base - low)[:, None] + spot, -1
    ).reshape(-1)
    ends = jnp.minimum(start + row_len.reshape(NX, -1), high[:, None])
    first = jnp.maximum(start, low[:, None])
    run_start = ((base - low)[:, None] + first).reshape(-1)
    run_end = run_start + jnp.maximum(ends - first, 0).reshape(-1)
    half = tokens // 2
    eighth = tokens // 8
    j = jnp.arange(tokens)
    owner_core = lax.axis_index("core") ^ (j // half)
    owner_y = (lax.axis_index("y") + (j % half) // eighth) % NY
    q = (owner_core * NY + owner_y) * eighth + j % eighth
    pick = (q[:, None] == place[None, :]).astype(BF)
    unpick = (place[:, None] == q[None, :]).astype(BF)
    rows_of = (run_start[None, :] <= q[:, None]) & (q[:, None] < run_end[None, :])
    return pick, unpick, rows_of


def gather_x(own):
    return jnp.concatenate([own] + [shift(own, "x", NX, k) for k in range(1, NX)], 0)


def forward(tokens, feats, weights, pick, packed_away):
    half = tokens // 2
    away = swap(dot(packed_away, weights, 1, 1, BF))
    packed_here = dot(pick[:half], feats, 1, 0, BF)
    here = dot(packed_here, weights, 1, 1) + away.astype(F32)
    return here, packed_here, packed_away


def sum_y(here):
    eighth = here.shape[0] // NY
    outputs = here[:eighth]
    parts = []
    for k in range(1, NY):
        block = here[k * eighth : (k + 1) * eighth].astype(BF)
        parts.append(shift(block, "y", NY, k))
        outputs = outputs + parts[-1].astype(F32)
    return outputs, parts[0]


def token_scale(rows_of, row_coef):
    return jnp.sum(jnp.where(rows_of, row_coef[None, :], 0.0), 1)[:, None]


def backward(grad_mine, packed_here, packed_away, weights, unpick, scale, own_scale):
    parts = [grad_mine] + [shift(grad_mine, "y", NY, -k) for k in range(1, NY)]
    grad_here = jnp.concatenate(parts, 0)
    grad_away = jnp.concatenate([swap(part) for part in parts], 0)
    half = grad_here.shape[0]
    packed_here = (packed_here.astype(F32) * scale[:half]).astype(BF)
    packed_away = (packed_away.astype(F32) * scale[half:]).astype(BF)
    proj = dot(grad_here, packed_here, 0, 0) + dot(grad_away, packed_away, 0, 0)
    grad_proj = lax.psum_scatter(proj.astype(BF), Z, scatter_dimension=0, tiled=True)
    back = jnp.concatenate(
        [dot(grad_here, weights, 1, 0, BF), dot(grad_away, weights, 1, 0, BF)], 0
    )
    per = unpick.shape[0] // NX
    total = dot(unpick[:per], back, 1, 0)
    for k in range(1, NX):
        part = dot(unpick[k * per : (k + 1) * per], back, 1, 0, BF)
        total = total + shift(part, "x", NX, -k).astype(F32)
    return (total * own_scale).astype(BF), grad_proj.astype(F32)


def body(
    cache_keys,
    cache_values,
    step_queries,
    step_keys,
    step_values,
    reward_head,
    lengths,
    assign,
    response_feats,
    out_proj,
    loss_probe,
):
    local_rows, slots, width_local = response_feats.shape
    total_rows = lengths.shape[0]
    shards = lax.axis_size(S)
    my_shard = lax.axis_index(S)
    zhi, xx, zlo = lax.axis_index("zhi"), lax.axis_index("x"), lax.axis_index("zlo")
    full = local_rows * slots
    few = 304
    section_full = NX * full
    section_few = 1024

    steps = jnp.arange(slots)
    targets = lax.dynamic_slice_in_dim(assign, my_shard * local_rows, local_rows) // local_rows
    goes = (targets[:, None] * slots + steps[None, :]).reshape(1, -1)
    placing = (jnp.arange(shards * slots)[:, None] == goes).astype(BF)
    outgoing = dot(placing, response_feats.reshape(full, width_local), 1, 0, BF)
    step_queries, outgoing = lax.optimization_barrier((step_queries, outgoing))
    incoming = lax.all_to_all(outgoing, S, split_axis=0, concat_axis=0, tiled=True)

    decoded = decode_rows(step_queries, cache_keys, cache_values, step_keys, step_values)
    head_terms = jnp.dot(
        decoded.reshape(local_rows * STEPS, width_local),
        reward_head,
        preferred_element_type=F32,
    )
    head_terms = head_terms.reshape(local_rows, STEPS).sum(1) / STEPS

    weights = lax.all_gather(after(out_proj, head_terms), Z, axis=0, tiled=True)

    ids = jnp.arange(NX * local_rows)
    shard = (zhi * NX + (xx - ids // local_rows) % NX) * 2 + zlo
    slot = shard * local_rows + ids % local_rows
    found = assign[None, :] == slot[:, None]
    all_rows = jnp.arange(total_rows)
    row_len = jnp.sum(jnp.where(found, lengths[None, :], 0), 1)
    from_shard = jnp.sum(jnp.where(found[:local_rows], (all_rows // local_rows)[None, :], 0), 1)
    own_len = row_len[:local_rows]
    own_ids = jnp.arange(local_rows)
    own_start = jnp.sum(
        jnp.where(own_ids[None, :] < own_ids[:, None], own_len[None, :], 0), 1
    )
    comes = from_shard[None, :] == jnp.arange(shards)[:, None]
    src_start = jnp.sum(jnp.where(comes, own_start[None, :], 0), 1)
    src_len = jnp.sum(jnp.where(comes, own_len[None, :], 0), 1)
    lies = jnp.where(
        steps[None, :] < src_len[:, None], src_start[:, None] + steps[None, :], -1
    ).reshape(1, -1)
    wants = jnp.where(
        steps[None, :] < own_len[:, None], own_start[:, None] + steps[None, :], -1
    ).reshape(-1, 1)
    picking = (jnp.arange(few)[:, None] == lies).astype(BF)
    leaving = (wants == jnp.arange(few)[None, :]).astype(BF)

    shard_len = jnp.sum(row_len.reshape(NX, local_rows), 1)
    capped = jnp.minimum(shard_len, few)
    blocks = jnp.arange(NX)
    ahead = jnp.sum(jnp.where(blocks[None, :] < blocks[:, None], capped[None, :], 0), 1)
    taken = jnp.clip(section_few - ahead, 0, capped)
    pick, unpick, rows_of = section_plan(
        section_few, few, slots, row_len, jnp.zeros_like(taken), taken
    )
    loads = jnp.sum(
        jnp.where(
            (assign // local_rows)[None, :] == jnp.arange(shards)[:, None], lengths[None, :], 0
        ),
        1,
    )
    sections = loads.reshape(4, NX, 2).sum(1)
    more = (jnp.max(loads) > few) | (jnp.max(sections) > section_few)
    row_rewards = lax.psum(head_terms, MP)
    pick, picking, incoming, row_rewards = lax.optimization_barrier(
        (pick, picking, incoming, row_rewards)
    )
    own = dot(picking, incoming, 1, 0, BF)
    rewards = share_small(after(row_rewards, own), S).reshape(-1)
    feats, weights = lax.optimization_barrier((gather_x(own), weights))
    packed_away = dot(pick[section_few // 2 :], feats, 1, 0, BF)
    packed_away, rewards = lax.optimization_barrier((packed_away, rewards))
    here, packed_here, packed_away = forward(
        section_few, feats, weights, pick, packed_away
    )

    outputs, first = sum_y(here)
    groups = total_rows // GROUP
    group_mean = rewards.reshape(GROUP, groups).mean(0)
    advantages = rewards - jnp.tile(group_mean, GROUP)
    row_adv = jnp.sum(jnp.where(found, advantages[None, :], 0.0), 1)
    row_coef = row_adv / row_len.astype(F32)
    per_shard = loss_probe.shape[0] // shards
    probe = lax.dynamic_index_in_dim(
        loss_probe.reshape(4, NX, 2 * per_shard), xx, 1, keepdims=False
    ).reshape(-1)

    def own_scale(count):
        spot = jnp.arange(count)[:, None]
        own_rows = (own_start[None, :] <= spot) & (spot < (own_start + own_len)[None, :])
        return token_scale(own_rows, row_coef[:local_rows])

    total, grad_proj = backward(
        grad_output(outputs, probe),
        packed_here,
        packed_away,
        weights,
        unpick,
        token_scale(rows_of, row_coef),
        own_scale(few),
    )
    total, more = lax.optimization_barrier((total, more))
    grad_own = dot(leaving, total, 1, 0, BF)

    def rest(args):
        grad_own, grad_proj, incoming, weights, row_coef, probe, lies, wants = args
        rest_tokens = section_full - section_few
        pick, unpick, rows_of = section_plan(
            rest_tokens, full, slots, row_len, taken, shard_len
        )
        picking = (jnp.arange(full)[:, None] == lies).astype(BF)
        leaving = (wants == jnp.arange(full)[None, :]).astype(BF)
        feats = gather_x(dot(picking, incoming, 1, 0, BF))
        packed_away = dot(pick[rest_tokens // 2 :], feats, 1, 0, BF)
        here, packed_here, packed_away = forward(
            rest_tokens, feats, weights, pick, packed_away
        )
        outputs, _ = sum_y(here)
        total, proj = backward(
            grad_output(outputs, probe),
            packed_here,
            packed_away,
            weights,
            unpick,
            token_scale(rows_of, row_coef),
            own_scale(full),
        )
        return grad_own + dot(leaving, total, 1, 0, BF), grad_proj + proj

    grad_own, grad_proj = lax.cond(
        more,
        rest,
        lambda args: (args[0], args[1]),
        (grad_own, grad_proj, incoming, weights, row_coef, probe, lies, wants),
    )
    grad_features = grad_own.reshape(local_rows, slots, width_local)
    return (advantages, grad_features, grad_proj)


def solution(mesh):
    fine = Mesh(
        mesh.devices.reshape(4, NX, 2, NY, 2), ("zhi", "x", "zlo", "y", "core")
    )
    rows3 = P(S, None, MP)
    placed = (
        rows3,
        rows3,
        rows3,
        rows3,
        rows3,
        P(MP),
        P(),
        P(),
        rows3,
        P(S, MP),
        P(),
    )
    return jax.shard_map(
        body,
        mesh=fine,
        in_specs=placed,
        out_specs=(P(), rows3, P(S, MP)),
        check_vma=False,
    )
```
